32 devices in a mesh: space: 8 (over y, x, core), chan: 4 (over z).
Axes of the slice: x: 2, y: 2, z: 4, core: 2. Of those that a mesh axis runs over, the one named last changes fastest.
Arguments:
- features: bfloat16 [64, 128, 512], P('space'), may hold values from -6 to 6
- voxel_mask: int32 [64, 512], P('space'), may hold values 0 or 1
- neighbors: int32 [64, 26], P('space'), may hold values from -1 to 15, as said below
- w_conv: bfloat16 [27, 128, 128], P(None, 'chan'), may hold values from -0.109375 to 0.109375
- w_down: bfloat16 [8, 256, 128], replicated, may hold values from -0.1875 to 0.1875
- coarse_owner: int32 [64, 1], P('space'), may hold values from 0 to 7; in each aligned block of 8 rows (0 to 7, 8 to 15, ...) at most 2 rows name the same one
- cotangent: bfloat16 [128, 256, 64], P('space', 'chan'), may hold values from -0.5 to 0.5
Outputs:
- coarse: bfloat16 [128, 256, 64], P('space', 'chan')
- grad_conv: float32 [27, 128, 128], P(None, 'chan')
- grad_down: float32 [8, 256, 128], P(None, 'chan')
The draws below stay inside these ranges and needn't reach their ends.
Inputs may be any that keep to these rules, and one draw needn't show every extreme that they name: `neighbors`: blocks 0 to 3 of a device lie in the first x-layer of its slab and the others in the second; slabs follow each other along x in device order, and block positions in a layer lie on a 8 x 8 grid in y and z. An entry is the neighbor's slot on the own device (below 8), 8 + i for slot 4 + i of the previous device, 12 + i for slot i of the next device, or -1 where the position is empty. `coarse_owner`: among the 8 blocks of one device at most 2 name the same owner.
All inputs are finite; a program needn't handle non-finite values. No bound on the sum of `voxel_mask` on one device may be relied on, other than what follows from the above.
Results may differ from the reference program's by a relative error of at most 0.001.
The reference program's roundings to bfloat16 on the way (of `masked`, `padded`, `hidden`, `dpiece` and `dpre`) count: a program that leaves them out, or rounds other values in their place, can miss the bound.
Values may be sent and summed in bfloat16 or wider, within the bound.
No kernel may reach another device: no remote copies, remote signals or barrier semaphores. Data moves between devices by JAX's collectives and lax.ppermute only.
A program may use at most 128 MiB of HBM per device.

```python
import math
import jax
import jax.numpy as jnp
import numpy as np
from jax import lax

C = 128
COUT = 256
E = 4
SIDE = 8
NB = 8
PEERS = 8
CAP = 2
BLOCKS = 64
SLOTS = 128
N_SPACE = 8


OFFSETS = [(step_x, step_y, step_z) for step_x in (-1, 0, 1) for step_y in (-1, 0, 1) for step_z in (-1, 0, 1)]


def draw_neighbors(key, part):
    devices = BLOCKS // NB
    cell_count = SIDE * SIDE
    layer_keys = jax.random.split(key, devices * 2)
    orders = jax.vmap(lambda layer_key: jax.random.permutation(layer_key, cell_count))(layer_keys)
    placed = orders[:, :E].astype(jnp.int32)
    lookup = jnp.full((devices * 2, cell_count), -1, jnp.int32)
    row_ids = jnp.arange(devices * 2, dtype=jnp.int32)[:, None]
    slot_values = jnp.broadcast_to(jnp.arange(E, dtype=jnp.int32)[None, :], (devices * 2, E))
    lookup = lookup.at[row_ids, placed].set(slot_values)
    lookup = lookup.reshape(devices, 2, cell_count)
    placed = placed.reshape(devices, 2, E)
    cell_y = placed // SIDE
    cell_z = placed % SIDE
    device_ids = jnp.arange(devices, dtype=jnp.int32)[:, None, None]
    layer_ids = jnp.arange(2, dtype=jnp.int32)[None, :, None]
    columns = []
    for step_x, step_y, step_z in OFFSETS:
        if (step_x, step_y, step_z) == (0, 0, 0):
            continue
        target = layer_ids + step_x
        moved_by = jnp.where(target < 0, -1, jnp.where(target > 1, 1, 0))
        target_device = device_ids + moved_by
        target_layer = target - 2 * moved_by
        near_y = cell_y + step_y
        near_z = cell_z + step_z
        inside = (target_device >= 0) & (target_device < devices) & (near_y >= 0) & (near_y < SIDE) & (near_z >= 0) & (near_z < SIDE)
        cell_index = jnp.clip(near_y, 0, SIDE - 1) * SIDE + jnp.clip(near_z, 0, SIDE - 1)
        found_slot = lookup[jnp.clip(target_device, 0, devices - 1), target_layer, cell_index]
        slot_id = jnp.where(moved_by == 0, target_layer * E + found_slot, jnp.where(moved_by < 0, NB + found_slot, NB + E + found_slot))
        slot_id = jnp.where(inside & (found_slot >= 0), slot_id, -1)
        columns.append(jnp.broadcast_to(slot_id, (devices, 2, E)).reshape(devices * 2 * E))
    return jnp.stack(columns, axis=1).astype(jnp.int32)


def touch_ends(entries, key, least, top_value):
    index_at = [jax.random.randint(jax.random.fold_in(key, axis), (), 0, length) for axis, length in enumerate(entries.shape)]
    widest = entries.shape.index(max(entries.shape))
    beside = index_at[:widest] + [(index_at[widest] + 1) % entries.shape[widest]] + index_at[widest + 1:]
    return entries.at[tuple(index_at)].set(least).at[tuple(beside)].set(top_value)


def levels(own_key, shape, cuts, least, top_value):
    factor_of, own = 1.0, jax.random.fold_in(own_key, 6)
    for dim, blocks in cuts:
        heights = jnp.exp(jax.random.uniform(jax.random.fold_in(own, dim), (blocks,), jnp.float32, least / len(cuts), top_value / len(cuts)))
        factor_of = factor_of * jnp.repeat(heights, shape[dim] // blocks).reshape([-1 if axis == dim else 1 for axis in range(len(shape))])
    return factor_of


def assign_block(stream_key, own, number, rows, count, top, limit, lean):
    ranking = jax.random.permutation(stream_key, count)
    heavy_load, common = shares(count, rows * top, limit, lean, True), shares(count, rows * top, limit, lean, False)
    places = jnp.arange(count)

    def named(lengths, offset_by):
        used = int((lengths > 0).sum())
        fixed = max(1, used // 4)
        moved = fixed + (places - fixed + offset_by * (used - fixed)) % max(1, count - fixed)
        return jnp.zeros((count,), jnp.int32).at[ranking[jnp.where(places < fixed, places, moved)]].set(jnp.asarray(lengths, jnp.int32))

    lengths = jnp.where(number % 4 == 0, named(heavy_load, number // 4), named(common, number - number // 4 - 1))
    mixed = jax.random.permutation(jax.random.fold_in(own, 3), count)
    source_of, receiver = mixed[0:count // 2 * 2:2], mixed[1:count // 2 * 2:2]
    margin = jnp.minimum(lengths[source_of] - 1, limit - lengths[receiver]) // 2
    margin = jnp.where((source_of == ranking[0]) | (receiver == ranking[0]) | (lengths[receiver] == 0), 0, jnp.maximum(margin, 0))
    moved = jax.random.randint(jax.random.fold_in(own, 4), (count // 2,), 0, 1 << 20) % (margin + 1)
    lengths = lengths.at[source_of].add(-moved).at[receiver].add(moved)
    items = jnp.searchsorted(jnp.cumsum(lengths), jnp.arange(rows * top), side="right").astype(jnp.int32)
    table = items.reshape(top, rows).T
    table = table[jax.random.permutation(jax.random.fold_in(own, 1), rows)]
    offset_by = jax.random.randint(jax.random.fold_in(own, 2), (rows, 1), 0, top)
    return jnp.take_along_axis(table, (jnp.arange(top)[None, :] + offset_by) % top, axis=1)


def shares(count, total, most, lean, full):
    portions = [(1 << 20) // math.isqrt(grade ** lean) + 1 for grade in range(1, count + 1)]
    largest = most if full else min(most, max(-(-total // count), total * portions[0] // sum(portions)))
    least = 1 if total - largest >= count - 1 else 0
    holding, surplus = [largest] + [least] * (count - 1), total - largest - least * (count - 1)
    while surplus > 0:
        free = [i for i in range(1, count) if holding[i] < largest] or [i for i in range(1, count) if holding[i] < most]
        pool, remaining = sum([portions[i] for i in free]), surplus
        for i in free:
            more = min(most - holding[i], max(1, remaining * portions[i] // pool), surplus)
            holding[i] = holding[i] + more
            surplus = surplus - more
    return np.array(holding)


def bell_draw(key, shape, width, most, cuts=(), kind=jnp.bfloat16):
    loudness = levels(key, shape, cuts, -0.22, 0.18) if cuts else 1.0
    array = jax.random.normal(key, shape, jnp.float32) * width * loudness
    return jnp.minimum(jnp.maximum(array, -most), most).astype(kind)


def setup_inputs(seed: int = 0) -> dict:
    seeds = jax.random.split(jax.random.key(seed), 8)
    features = bell_draw(seeds[0], (BLOCKS, C, 512), 1.0, 6.0, ((0, 8),))
    voxel_mask = touch_ends((jax.random.randint(seeds[1], (BLOCKS, 512), 0, 2) < 1).astype(jnp.int32), jax.random.fold_in(seeds[1], 1), 0, 1)
    neighbors = draw_neighbors(jax.random.fold_in(seeds[7], 71), 0)
    w_conv = bell_draw(seeds[3], (27, C, C), (27 * C) ** -0.5, 0.109375, ((1, 4),))
    w_down = bell_draw(seeds[4], (8, COUT, C), (8 * C) ** -0.5, 0.1875)
    coarse_owner_keys = jax.random.split(jax.random.fold_in(seeds[5], 1), BLOCKS // NB)
    coarse_owner_turns = jax.random.permutation(jax.random.fold_in(seeds[5], 3), BLOCKS // NB)
    coarse_owner = jax.vmap(lambda own, number: assign_block(jax.random.fold_in(seeds[5], 2), own, number, NB, N_SPACE, 1, CAP, 2))(coarse_owner_keys, coarse_owner_turns).reshape((BLOCKS, 1))
    cotangent = bell_draw(seeds[6], (SLOTS, COUT, 64), (0.25 / BLOCKS ** 0.5), 0.5, ((0, 8), (1, 4)))
    return {"features": features, "voxel_mask": voxel_mask, "neighbors": neighbors, "w_conv": w_conv, "w_down": w_down, "coarse_owner": coarse_owner, "cotangent": cotangent}


OFFSETS = [(step_x, step_y, step_z) for step_x in (-1, 0, 1) for step_y in (-1, 0, 1) for step_z in (-1, 0, 1)]
CENTER = 13

def block_faces(blocks):
    block_count, channels = (blocks.shape[0], blocks.shape[1])
    cube_grid = blocks.reshape(block_count, channels, 8, 8, 8)
    face_list = [cube_grid[:, :, 0], cube_grid[:, :, 7], cube_grid[:, :, :, 0], cube_grid[:, :, :, 7], cube_grid[:, :, :, :, 0], cube_grid[:, :, :, :, 7]]
    return jnp.stack([one_face.reshape(block_count, channels, 64) for one_face in face_list], axis=1)

def neighbor_piece(lookup_rows, neighbor_ids, offset, slot_count):
    lead_axis = [which_axis for which_axis in range(3) if offset[which_axis] != 0][0]
    face_index = 2 * lead_axis + (1 if offset[lead_axis] < 0 else 0)
    row_index = jnp.where(neighbor_ids < 0, 7 * slot_count, jnp.where(neighbor_ids < slot_count, 6 * neighbor_ids + face_index, 5 * slot_count + neighbor_ids)).astype(jnp.int32)
    picked = jnp.take(lookup_rows, row_index, axis=0)
    picked = picked.reshape(picked.shape[0], picked.shape[1], 8, 8)
    other_axes = [which_axis for which_axis in range(3) if which_axis != lead_axis]
    for position_dim, which_axis in enumerate(other_axes):
        if offset[which_axis] == 1:
            picked = lax.slice_in_dim(picked, 0, 1, axis=2 + position_dim)
        elif offset[which_axis] == -1:
            picked = lax.slice_in_dim(picked, 7, 8, axis=2 + position_dim)
    return jnp.expand_dims(picked, 2 + lead_axis)

def padded_blocks(lookup_rows, neighbors, own_blocks, slot_total):
    block_count, channels = (own_blocks.shape[0], own_blocks.shape[1])
    cube_grid = own_blocks.reshape(block_count, channels, 8, 8, 8)
    planes = []
    for plane_x in range(3):
        line_list = []
        for line_y in range(3):
            cell_list = []
            for cell_z in range(3):
                position = 9 * plane_x + 3 * line_y + cell_z
                if position == CENTER:
                    cell_list.append(cube_grid)
                else:
                    column = position if position < CENTER else position - 1
                    cell_list.append(neighbor_piece(lookup_rows, neighbors[:, column], OFFSETS[position], slot_total))
            line_list.append(jnp.concatenate(cell_list, axis=4))
        planes.append(jnp.concatenate(line_list, axis=3))
    return jnp.concatenate(planes, axis=2).reshape(block_count, channels, 1000)

def window_at(padded, position):
    step_x, step_y, step_z = OFFSETS[position]
    block_count, channels = (padded.shape[0], padded.shape[1])
    cube_grid = padded.reshape(block_count, channels, 10, 10, 10)
    piece = cube_grid[:, :, 1 + step_x:9 + step_x, 1 + step_y:9 + step_y, 1 + step_z:9 + step_z]
    return piece.reshape(block_count, channels, 512)

def conv_blocks(padded, weights):
    summed = None
    for position in range(27):
        product = jnp.einsum('oi,bit->bot', weights[position].astype(jnp.float32), window_at(padded, position).astype(jnp.float32))
        summed = product if summed is None else summed + product
    return summed

def conv_weight_grad(padded, grad_out):
    spread = grad_out.astype(jnp.float32)
    grads = []
    for position in range(27):
        grads.append(jnp.einsum('bot,bit->oi', spread, window_at(padded, position).astype(jnp.float32)))
    return jnp.stack(grads)

def down_forward(weights, hidden):
    kernel = weights.reshape(2, 2, 2, weights.shape[1], weights.shape[2]).astype(jnp.float32)
    octants = hidden.reshape(hidden.shape[0], hidden.shape[1], 4, 2, 4, 2, 4, 2).astype(jnp.float32)
    result = jnp.einsum('ijkcd,bdxiyjzk->cbxyz', kernel, octants)
    return result.reshape(weights.shape[1], hidden.shape[0], 64)

def down_grad_weight(dpiece, hidden):
    grid_piece = dpiece.reshape(dpiece.shape[0], dpiece.shape[1], 4, 4, 4).astype(jnp.float32)
    octants = hidden.reshape(hidden.shape[0], hidden.shape[1], 4, 2, 4, 2, 4, 2).astype(jnp.float32)
    result = jnp.einsum('cbxyz,bdxiyjzk->ijkcd', grid_piece, octants)
    return result.reshape(8, dpiece.shape[0], hidden.shape[1])

def down_grad_input(weights, dpiece):
    kernel = weights.reshape(2, 2, 2, weights.shape[1], weights.shape[2]).astype(jnp.float32)
    grid_piece = dpiece.reshape(dpiece.shape[0], dpiece.shape[1], 4, 4, 4).astype(jnp.float32)
    result = jnp.einsum('ijkcd,cbxyz->bdxiyjzk', kernel, grid_piece)
    return result.reshape(dpiece.shape[1], weights.shape[2], 512)

def routing_table(owner, peers, capacity):
    targets = jnp.arange(peers, dtype=jnp.int32)
    dest_hits = (owner[:, None] == targets[None, :]).astype(jnp.int32)
    earlier = jnp.cumsum(dest_hits, axis=0) - dest_hits
    dest_rank = lax.optimization_barrier(jnp.sum(earlier * dest_hits, axis=1))
    places = jnp.arange(capacity, dtype=jnp.int32)
    return (owner[None, None, :] == targets[:, None, None]) & (dest_rank[None, None, :] == places[None, :, None])

def reference(features, voxel_mask, neighbors, w_conv, w_down, coarse_owner, cotangent):
    mask_float = voxel_mask.astype(jnp.float32)[:, None, :]
    masked = (features.astype(jnp.float32) * mask_float).astype(jnp.bfloat16)
    device_blocks = masked.reshape(PEERS, NB, C, 512)
    bordered = jnp.pad(device_blocks, ((1, 1), (0, 0), (0, 0), (0, 0)))
    device_neighbors = neighbors.reshape(PEERS, NB, 26)
    device_owner = coarse_owner.reshape(PEERS, NB)
    device_mask = mask_float.reshape(PEERS, NB, 1, 512)
    cotangent_grid = cotangent.reshape(PEERS, PEERS, CAP, COUT, 64)

    def one_device(device):
        own_blocks = bordered[device + 1]
        before = bordered[device][E:]
        after = bordered[device + 2][:E]
        lookup_rows = jnp.concatenate([block_faces(own_blocks).reshape(6 * NB, C, 64), block_faces(before)[:, 1], block_faces(after)[:, 0], jnp.zeros((1, C, 64), own_blocks.dtype)])
        padded = padded_blocks(lookup_rows, device_neighbors[device], own_blocks, NB)
        conv_out = conv_blocks(padded, w_conv)
        keep_mask = device_mask[device]
        pre_act = own_blocks.astype(jnp.float32) + conv_out
        hidden = (keep_mask * jax.nn.silu(pre_act)).astype(jnp.bfloat16)
        down_out = down_forward(w_down, hidden)
        chosen = routing_table(device_owner[device], PEERS, CAP).astype(jnp.float32)
        pieces = lax.optimization_barrier(down_out.astype(jnp.bfloat16)).astype(jnp.float32)
        outgoing = jnp.einsum('drj,cjq->drcq', chosen, pieces).astype(jnp.bfloat16)
        returned = cotangent_grid[:, device].astype(jnp.float32)
        dpiece = jnp.einsum('drj,drcq->cjq', chosen, returned).astype(jnp.bfloat16)
        down_grad = down_grad_weight(dpiece, hidden)
        dhidden = down_grad_input(w_down, dpiece)
        sigmoid = jax.nn.sigmoid(pre_act)
        dpre = (dhidden * keep_mask * sigmoid * (1.0 + pre_act * (1.0 - sigmoid))).astype(jnp.bfloat16)
        conv_grad = conv_weight_grad(padded, dpre)
        return (outgoing, conv_grad, down_grad)
    outgoing, conv_grads, down_grads = lax.map(one_device, jnp.arange(PEERS, dtype=jnp.int32))
    coarse = jnp.transpose(outgoing, (1, 0, 2, 3, 4)).reshape(SLOTS, COUT, 64)
    return (coarse, lax.optimization_barrier(jnp.sum(conv_grads, axis=0)), lax.optimization_barrier(jnp.sum(down_grads, axis=0)))
```

```python
import functools

import jax
import jax.numpy as jnp
import numpy as np
from jax import lax
from jax.experimental import pallas as pl
from jax.experimental.pallas import tpu as pltpu
from jax.sharding import PartitionSpec as P

F32 = jnp.float32
BF16 = jnp.bfloat16
SIGNS = (-1, 0, 1)
LANES = 128
NT = (((1,), (1,)), ((), ()))
TN = (((0,), (0,)), ((), ()))
VMEM_LIMIT = 60 * 1024 * 1024


def vmem():
    return pl.BlockSpec(memory_space=pltpu.VMEM)


def smem():
    return pl.BlockSpec(memory_space=pltpu.SMEM)


def rim_lane(cell_y, cell_z):
    if 0 <= cell_y < 8 and 0 <= cell_z < 8:
        return 8 * cell_y + cell_z
    if 0 <= cell_z < 8:
        return 64 + 8 * (cell_y > 0) + cell_z
    if 0 <= cell_y < 8:
        return 80 + 8 * (cell_z > 0) + cell_y
    return 96 + 2 * (cell_y > 0) + (cell_z > 0)


def edge_table():
    table = np.zeros((9, LANES, LANES), np.float32)
    for place, (step_y, step_z) in enumerate((a, b) for a in SIGNS for b in SIGNS):
        for cell_y in range(8):
            for cell_z in range(8):
                far_y, far_z = cell_y + 8 * step_y, cell_z + 8 * step_z
                if -1 <= far_y <= 8 and -1 <= far_z <= 8:
                    table[place, 8 * cell_y + cell_z, rim_lane(far_y, far_z)] = 1
    return table


def shift_table():
    table = np.zeros((9, 2, 64, 2, LANES), np.float32)
    for place, (step_y, step_z) in enumerate((a, b) for a in SIGNS for b in SIGNS):
        for cell_y in range(8):
            for cell_z in range(8):
                lane = rim_lane(cell_y + step_y, cell_z + step_z)
                for plane in range(2):
                    table[place, plane, 8 * cell_y + cell_z, plane, lane] = 1
    return table.reshape(9 * 2 * 64, 2 * LANES)


def octant_table():
    table = np.zeros((8, 8, 8, 8, 2, 64), np.float32)
    for x in range(8):
        for y in range(8):
            for z in range(8):
                octant = 4 * (x % 2) + 2 * (y % 2) + z % 2
                table[x, y, z, octant, :, 16 * (x // 2) + 4 * (y // 2) + z // 2] = 1
    return table.reshape(512, 8 * LANES)


def ranks(owner_ref, block):
    place = jnp.int32(0)
    for earlier in range(block):
        place = place + (owner_ref[earlier, 0] == owner_ref[block, 0]).astype(jnp.int32)
    return place


def pick_kernel(capacity, owner_ref, returned_ref, out_ref):
    blocks = owner_ref.shape[0]
    for pair in range(blocks // 2):
        rows = []
        for block in (2 * pair, 2 * pair + 1):
            slot = owner_ref[block, 0] * capacity + ranks(owner_ref, block)
            rows.append(returned_ref[slot].astype(F32))
        out_ref[:, pair * LANES : (pair + 1) * LANES] = jnp.concatenate(rows, axis=1).astype(BF16)


def route_kernel(capacity, owner_ref, *refs):
    out_ref = refs[-1]
    blocks = owner_ref.shape[0]
    total = refs[0][...]
    for ref in refs[1:-1]:
        total = total + ref[...]
    out_ref[...] = jnp.zeros_like(out_ref)
    for block in range(blocks):
        slot = owner_ref[block, 0] * capacity + ranks(owner_ref, block)
        piece = total[:, block * 64 : (block + 1) * 64].astype(BF16)
        out_ref[slot] = piece


def main_kernel(
    shards,
    partner,
    split,
    nbr_ref,
    at_ref,
    feat_ref,
    mask_ref,
    prev_ref,
    next_ref,
    wconv_ref,
    wdown_ref,
    edge_ref,
    shift_ref,
    octant_ref,
    *refs,
):
    dps = refs[:shards]
    refs = refs[shards:]
    outs = refs[:3]
    planes, patches, weights, pre_s, hidden_s, octs, spread, pieces_s, dp_s, dh_s, dhi, dlo, d3, grads = refs[3:]
    blocks, channels = feat_ref.shape[0], feat_ref.shape[1]
    edge = blocks // 2
    width = wconv_ref.shape[1]
    total = wdown_ref.shape[1]
    share = total // shards
    me = at_ref[0]
    lane = lax.broadcasted_iota(jnp.int32, (channels, LANES), 1)
    low = lane < 64
    halo = 10 * blocks

    zero_plane = jnp.zeros((channels, LANES), BF16)
    for block in range(blocks):
        keep = mask_ref[block : block + 1, :].astype(F32)
        masked = feat_ref[block].astype(F32) * keep
        planes[10 * block] = zero_plane
        planes[10 * block + 9] = zero_plane
        for pair in range(4):
            tile = masked[:, pair * LANES : (pair + 1) * LANES]
            planes[10 * block + 1 + 2 * pair] = jnp.where(low, tile, 0.0).astype(BF16)
            planes[10 * block + 2 + 2 * pair] = jnp.where(low, pltpu.roll(tile, 64, 1), 0.0).astype(BF16)
    for i in range(edge):
        planes[halo + i] = zero_plane
        planes[halo + edge + i] = zero_plane
        planes[halo + i, :, 0:64] = prev_ref[i]
        planes[halo + edge + i, :, 0:64] = next_ref[i]

    def rim(item, carry):
        block = item // 26
        column = item - block * 26
        source = nbr_ref[block, column]

        @pl.when(source >= 0)
        def _():
            position = column + (column >= 13).astype(jnp.int32)
            step_x = position // 9 - 1
            table = edge_ref[position - 9 * (step_x + 1)]

            @pl.when(step_x == 0)
            def _():
                cells = planes[pl.ds(source * 10 + 1, 8)].reshape(8 * channels, LANES)
                moved = jnp.dot(cells, table, preferred_element_type=F32).astype(BF16)
                planes[pl.ds(block * 10 + 1, 8)] += moved.reshape(8, channels, LANES)

            @pl.when(step_x != 0)
            def _():
                own = source * 10 + jnp.where(step_x < 0, 8, 1)
                cells = planes[jnp.where(source < blocks, own, halo + source - blocks)]
                moved = jnp.dot(cells, table, preferred_element_type=F32).astype(BF16)
                planes[block * 10 + jnp.where(step_x < 0, 0, 9)] += moved

        return carry

    lax.fori_loop(0, blocks * 26, rim, 0)

    for k in range(27):
        weights[(k // 9) * width : (k // 9 + 1) * width, (k % 9) * channels : (k % 9 + 1) * channels] = wconv_ref[k]

    def patch(item, carry):
        block = 2 * (item // 5)
        plane = 2 * (item % 5)
        first, second = block * 10 + plane, block * 10 + 10 + plane
        source = jnp.concatenate(
            [
                jnp.concatenate([planes[first], planes[first + 1]], axis=1),
                jnp.concatenate([planes[second], planes[second + 1]], axis=1),
            ],
            axis=0,
        )
        window = lax.dot_general(shift_ref[...], source, NT, preferred_element_type=F32).astype(BF16)
        for j in range(9):
            for half in range(2):
                row = pl.multiple_of((first + 10 * half) * 64, 128)
                patches[pl.ds(row, 128), j * channels : (j + 1) * channels] = window[
                    j * 128 : (j + 1) * 128, half * channels : (half + 1) * channels
                ]
        return carry

    lax.fori_loop(0, 5 * (blocks // 2), patch, 0)

    own_rows = pl.ds(pl.multiple_of(me * width, width), width)

    def forward(block, carry):
        rows = pl.ds(pl.multiple_of(block * 640, 128), 640)
        sums = lax.dot_general(weights[...], patches[rows, :], NT, preferred_element_type=F32)
        keep = mask_ref[pl.ds(block, 1), :].astype(F32)
        pre = (
            feat_ref[block, own_rows, :].astype(F32) * keep
            + sums[:width, 0:512]
            + pltpu.roll(sums[width : 2 * width], 640 - 64, 1)[:, 0:512]
            + sums[2 * width :, 128:640]
        )
        here = pl.ds(pl.multiple_of(block * width, width), width)
        pre_s[here, :] = pre
        hidden_s[here, :] = (keep * (pre * (1.0 / (1.0 + jnp.exp(-pre))))).astype(BF16)
        return carry

    lax.fori_loop(0, blocks, forward, 0)

    split_up = jnp.dot(hidden_s[...], octant_ref[...], preferred_element_type=F32)
    low_w = low[:width]
    spread[...] = jnp.zeros_like(spread)
    for octant in range(8):
        for pair in range(blocks // 2):
            even = split_up[2 * pair * width : (2 * pair + 1) * width, octant * LANES : (octant + 1) * LANES]
            odd = split_up[(2 * pair + 1) * width : (2 * pair + 2) * width, octant * LANES : (octant + 1) * LANES]
            tile = jnp.where(low_w, even, odd).astype(BF16)
            octs[octant * width : (octant + 1) * width, pair * LANES : (pair + 1) * LANES] = tile
            spread[pl.ds(pl.multiple_of(octant * channels + me * width, width), width), pair * LANES : (pair + 1) * LANES] = tile
    down_weights = jnp.concatenate([wdown_ref[octant] for octant in range(8)], axis=1)
    pieces_s[...] = jnp.dot(down_weights, spread[...], preferred_element_type=F32)
    for k in range(shards):
        theirs = pl.multiple_of(partner(me, k) * share, share)
        outs[0][k] = pieces_s[pl.ds(theirs, share), :]
        dp_s[pl.ds(theirs, share), :] = dps[k][...]

    for octant in range(8):
        dh_s[octant] = lax.dot_general(wdown_ref[octant], dp_s[...], TN, preferred_element_type=F32)
    for octant in range(8):
        for pair in range(blocks // 2):
            tile = dh_s[octant, own_rows, pair * LANES : (pair + 1) * LANES]
            high = tile.astype(BF16).astype(F32)
            rest = tile - high
            lanes = slice(octant * LANES, (octant + 1) * LANES)
            even = slice(2 * pair * width, (2 * pair + 1) * width)
            odd = slice((2 * pair + 1) * width, (2 * pair + 2) * width)
            dhi[even, lanes] = jnp.where(low_w, high, 0.0).astype(BF16)
            dhi[odd, lanes] = jnp.where(low_w, 0.0, high).astype(BF16)
            dlo[even, lanes] = jnp.where(low_w, rest, 0.0).astype(BF16)
            dlo[odd, lanes] = jnp.where(low_w, 0.0, rest).astype(BF16)
    dhidden = lax.dot_general(dhi[...], octant_ref[...], NT, preferred_element_type=F32)
    dhidden = dhidden + lax.dot_general(dlo[...], octant_ref[...], NT, preferred_element_type=F32)

    blank = jnp.zeros((width, LANES), F32)
    for block in range(blocks):
        rows = slice(block * width, (block + 1) * width)
        pre = pre_s[rows, :]
        keep = mask_ref[block : block + 1, :].astype(F32)
        gate = 1.0 / (1.0 + jnp.exp(-pre))
        dpre = dhidden[rows] * keep * gate * (1.0 + pre * (1.0 - gate))
        at = block * 640
        d3[0:width, at : at + 512] = dpre.astype(BF16)
        d3[0:width, at + 512 : at + 640] = blank.astype(BF16)
        d3[width : 2 * width, at : at + 640] = pltpu.roll(jnp.concatenate([dpre, blank], axis=1), 64, 1).astype(BF16)
        d3[2 * width :, at : at + 128] = blank.astype(BF16)
        d3[2 * width :, at + 128 : at + 640] = dpre.astype(BF16)

    down_grad = lax.dot_general(dp_s[...], octs[...], NT, preferred_element_type=F32)
    if split is None:
        for j in range(9):
            part = jnp.dot(d3[...], patches[:, j * channels : (j + 1) * channels], preferred_element_type=F32)
            for dx in range(3):
                outs[1][9 * dx + j] = part[dx * width : (dx + 1) * width]
        grads[0:total] = down_grad[:, 0:LANES]
        grads[total : 2 * total] = down_grad[:, LANES:]
        for k in range(shards):
            theirs = pl.multiple_of(partner(me, k) * share, share)
            outs[2][k, :, 0:LANES] = grads[pl.ds(theirs, share), :]
            outs[2][k, :, LANES:] = grads[pl.ds(total + theirs, share), :]
        return
    chips, conv_rows, down_rows = split
    chunk = conv_rows + shards * down_rows
    for j in range(9):
        part = jnp.dot(d3[...], patches[:, j * channels : (j + 1) * channels], preferred_element_type=F32)
        for dx in range(3):
            first = (9 * dx + j) * width
            for row in range(first, first + width, 8):
                at = (row // conv_rows) * chunk + row % conv_rows
                grads[at : at + 8] = part[dx * width + row - first : dx * width + row - first + 8]
    for row in range(27 * width, 2 * chips * conv_rows, 8):
        at = (row // conv_rows) * chunk + row % conv_rows
        grads[at : at + 8] = jnp.zeros((8, LANES), F32)
    down_s = pieces_s
    down_s[:, 0 : 2 * LANES] = down_grad
    for k in range(shards):
        theirs = partner(me, k) * share
        for part in range(2 * chips):
            row = part * down_rows
            source = pl.ds(pl.multiple_of(theirs + row % share, 8), down_rows)
            at = part * chunk + conv_rows + k * down_rows
            grads[at : at + down_rows] = down_s[source, (row // share) * LANES : (row // share + 1) * LANES]
    core, chip = at_ref[1], at_ref[2]
    for k in range(chips):
        theirs = chip ^ k
        outs[1][k] = grads[pl.ds(pl.multiple_of((2 * theirs + core) * chunk, 8), chunk), :]
        outs[2][k] = grads[pl.ds(pl.multiple_of((2 * theirs + 1 - core) * chunk, 8), chunk), :]


def finish_kernel(shards, partner, split, at_ref, own_ref, other_ref, conv_ref, down_ref, conv_s, down_s):
    chips, conv_rows, down_rows = split
    me, core, chip = at_ref[0], at_ref[1], at_ref[2]
    share = down_ref.shape[1]
    width = conv_ref.shape[1]
    for side, ref in enumerate((own_ref, other_ref)):
        for k in range(chips):
            part = 2 * (chip ^ k) + (core if side == 0 else 1 - core)
            conv_s[pl.ds(pl.multiple_of(part * conv_rows, 8), conv_rows), :] = ref[k, :conv_rows]
            for source in range(shards):
                row = conv_rows + source * down_rows
                at = pl.multiple_of(part * down_rows, 8)
                down_s[source, pl.ds(at, down_rows), :] = ref[k, row : row + down_rows]
    for k in range(27):
        conv_ref[k] = conv_s[k * width : (k + 1) * width]
    group = lax.broadcasted_iota(jnp.int32, (share, LANES), 1) // width
    for octant in range(8):
        result = jnp.zeros((share, LANES), F32)
        for k in range(shards):
            source = partner(me, k)
            tile = down_s[k, (octant // 4) * share : (octant // 4 + 1) * share, :]
            turned = pltpu.roll(tile, ((source - octant % 4 + 4) % 4) * width, 1)
            result = jnp.where(group == source, turned, result)
        down_ref[octant] = result


def permute(values, axis, pairs):
    return lax.ppermute(values, axis, pairs)


def exchange(values, axis, step):
    count = lax.axis_size(axis)
    return lax.ppermute(values, axis, [(i, i ^ step) for i in range(count)])


def local(features, voxel_mask, neighbors, w_conv, w_down, coarse_owner, cotangent):
    blocks, channels = features.shape[0], features.shape[1]
    edge = blocks // 2
    peers = lax.axis_size("space")
    shards = lax.axis_size("chan")
    width = w_conv.shape[1]
    total = w_down.shape[1]
    share = total // shards
    capacity = cotangent.shape[0] // peers
    me = lax.axis_index("chan").astype(jnp.int32)
    spot = lax.axis_index("space").astype(jnp.int32)
    at = jnp.stack([me, spot % 2, spot // 2])

    def partner(index, k):
        return index ^ k

    head = features[:edge, :, :64] * voxel_mask[:edge, None, :64].astype(BF16)
    tail = features[edge:, :, 448:] * voxel_mask[edge:, None, 448:].astype(BF16)
    ends = peers - 1
    before = lax.ppermute(tail, "space", [(i, i + 1) for i in range(ends)])
    after = lax.ppermute(head, "space", [(i + 1, i) for i in range(ends)])

    returned = lax.all_to_all(
        cotangent.reshape(peers, capacity * share, 64), "space", split_axis=0, concat_axis=0, tiled=True
    ).reshape(peers * capacity, share, 64)
    lanes = blocks * 64
    dpiece = pl.pallas_call(
        functools.partial(pick_kernel, capacity),
        out_shape=jax.ShapeDtypeStruct((share, lanes), BF16),
        in_specs=[smem(), vmem()],
        out_specs=vmem(),
    )(coarse_owner, returned)
    dpieces = [dpiece] + [exchange(dpiece, "chan", k) for k in range(1, shards)]

    down_rows = 2 * share // peers
    chips = peers // 2
    split = None
    if peers & ends == 0 and down_rows % 8 == 0 and share % down_rows == 0:
        conv_rows = -(-27 * width // (8 * peers)) * 8
        split = (chips, conv_rows, down_rows)
        chunk = conv_rows + shards * down_rows
        grad_shapes = [(chips, chunk, LANES)] * 2
        grad_rows = peers * chunk
    else:
        grad_shapes = [(27, width, channels), (shards, share, 2 * LANES)]
        grad_rows = 2 * total

    pieces, first, second = pl.pallas_call(
        functools.partial(main_kernel, shards, partner, split),
        out_shape=[jax.ShapeDtypeStruct(s, F32) for s in [(shards, share, lanes)] + grad_shapes],
        in_specs=[smem(), smem()] + [vmem()] * (9 + shards),
        out_specs=[vmem()] * 3,
        scratch_shapes=[
            pltpu.VMEM((11 * blocks, channels, LANES), BF16),
            pltpu.VMEM((blocks * 640, 9 * channels), BF16),
            pltpu.VMEM((3 * width, 9 * channels), BF16),
            pltpu.VMEM((blocks * width, 512), F32),
            pltpu.VMEM((blocks * width, 512), BF16),
            pltpu.VMEM((8 * width, lanes), BF16),
            pltpu.VMEM((8 * channels, lanes), BF16),
            pltpu.VMEM((total, lanes), F32),
            pltpu.VMEM((total, lanes), BF16),
            pltpu.VMEM((8, channels, lanes), F32),
            pltpu.VMEM((blocks * width, 8 * LANES), BF16),
            pltpu.VMEM((blocks * width, 8 * LANES), BF16),
            pltpu.VMEM((3 * width, blocks * 640), BF16),
            pltpu.VMEM((grad_rows, LANES), F32),
        ],
        compiler_params=pltpu.CompilerParams(vmem_limit_bytes=VMEM_LIMIT),
    )(
        neighbors,
        at,
        features,
        voxel_mask,
        before,
        after,
        w_conv,
        w_down,
        jnp.asarray(edge_table(), BF16),
        jnp.asarray(shift_table(), BF16),
        jnp.asarray(octant_table(), BF16),
        *dpieces,
    )

    parts = [pieces[0]] + [exchange(pieces[k], "chan", k) for k in range(1, shards)]
    outgoing = pl.pallas_call(
        functools.partial(route_kernel, capacity),
        out_shape=jax.ShapeDtypeStruct((peers * capacity, share, 64), BF16),
        in_specs=[smem()] + [vmem()] * shards,
        out_specs=vmem(),
    )(coarse_owner, *parts)
    coarse = lax.all_to_all(
        outgoing.reshape(peers, capacity * share, 64), "space", split_axis=0, concat_axis=0, tiled=True
    ).reshape(peers * capacity, share, 64)

    if split is None:
        conv_sum = lax.psum(first, "space")
        parts = [second[0]] + [exchange(second[k], "chan", k) for k in range(1, shards)]
        down_parts = jnp.stack(parts)
        order = jnp.arange(shards, dtype=jnp.int32) ^ me
        down_parts = jnp.take(down_parts, order, axis=0).reshape(shards, share, 8, width)
        down_sum = lax.psum(down_parts.transpose(2, 1, 0, 3).reshape(8, share, shards * width), "space")
        return coarse, conv_sum, down_sum

    chips, conv_rows, down_rows = split
    halves = first + exchange(second, "space", 1)
    mine = halves[0]
    for k in range(1, chips):
        mine = mine + exchange(halves[k], "space", 2 * k)
    downs = [mine[conv_rows + k * down_rows : conv_rows + (k + 1) * down_rows] for k in range(shards)]
    downs = [downs[0]] + [exchange(downs[k], "chan", k) for k in range(1, shards)]
    mine = jnp.concatenate([mine[:conv_rows]] + downs)
    all_mine = jnp.stack([mine] + [exchange(mine, "space", 2 * k) for k in range(1, chips)])
    all_other = exchange(all_mine, "space", 1)
    conv_sum, down_sum = pl.pallas_call(
        functools.partial(finish_kernel, shards, partner, split),
        out_shape=[
            jax.ShapeDtypeStruct((27, width, channels), F32),
            jax.ShapeDtypeStruct((8, share, channels), F32),
        ],
        in_specs=[smem(), vmem(), vmem()],
        out_specs=[vmem()] * 2,
        scratch_shapes=[
            pltpu.VMEM((peers * conv_rows, LANES), F32),
            pltpu.VMEM((shards, 2 * share, LANES), F32),
        ],
    )(at, all_mine, all_other)
    return coarse, conv_sum, down_sum


def solution(mesh):
    in_specs = (
        P("space", None, None),
        P("space", None),
        P("space", None),
        P(None, "chan", None),
        P(),
        P("space", None),
        P("space", "chan", None),
    )
    out_specs = (P("space", "chan", None), P(None, "chan", None), P(None, "chan", None))
    return jax.shard_map(local, mesh=mesh, in_specs=in_specs, out_specs=out_specs, check_vma=False)
```

```python
import functools

import jax
import jax.numpy as jnp
import numpy as np
from jax import lax
from jax.experimental import pallas as pl
from jax.experimental.pallas import tpu as pltpu
from jax.sharding import PartitionSpec as P

F32 = jnp.float32
BF16 = jnp.bfloat16
SIGNS = (-1, 0, 1)
LANES = 128
NT = (((1,), (1,)), ((), ()))
TN = (((0,), (0,)), ((), ()))
MIB = 1024 * 1024
PLANE = 80
STRIDE = 896
SPAN = 640


def vmem():
    return pl.BlockSpec(memory_space=pltpu.VMEM)


def smem():
    return pl.BlockSpec(memory_space=pltpu.SMEM)


def rim_lane(cell_y, cell_z):
    if 0 <= cell_y < 8 and 0 <= cell_z < 8:
        return 8 * cell_y + cell_z
    if 0 <= cell_z < 8:
        return 64 + 8 * (cell_y > 0) + cell_z
    if 0 <= cell_y < 8:
        return 80 + 8 * (cell_z > 0) + cell_y
    return 96 + 2 * (cell_y > 0) + (cell_z > 0)


def edge_table():
    table = np.zeros((10, LANES, LANES), np.float32)
    for place, (step_y, step_z) in enumerate((a, b) for a in SIGNS for b in SIGNS):
        for cell_y in range(8):
            for cell_z in range(8):
                far_y, far_z = cell_y + 8 * step_y, cell_z + 8 * step_z
                if -1 <= far_y <= 8 and -1 <= far_z <= 8:
                    table[place, 8 * cell_y + cell_z, rim_lane(far_y, far_z)] = 1
    return table


def shift_table():
    table = np.zeros((3, 2, 10, 8, 2, LANES), np.float32)
    for place, step_z in enumerate(SIGNS):
        for cell_y in range(10):
            for cell_z in range(8):
                for plane in range(2):
                    table[place, plane, cell_y, cell_z, plane, rim_lane(cell_y - 1, cell_z + step_z)] = 1
    return table.reshape(3 * 2 * PLANE, 2 * LANES)


def spread_table():
    table = np.zeros((8, 64, 8, PLANE), np.float32)
    for x in range(8):
        for cell in range(64):
            table[x, cell, x, cell] = 1
    return table.reshape(512, SPAN)


def octant_table():
    table = np.zeros((8, PLANE, 8, 2, 64), np.float32)
    for x in range(8):
        for y in range(8):
            for z in range(8):
                octant = 4 * (x % 2) + 2 * (y % 2) + z % 2
                table[x, 8 * y + z, octant, :, 16 * (x // 2) + 4 * (y // 2) + z // 2] = 1
    return table.reshape(SPAN, 8 * LANES)


def low_half(rows):
    return lax.broadcasted_iota(jnp.int32, (rows, LANES), 1) < 64


def swap_halves(tile):
    return pltpu.roll(tile, 64, 1)


def prepare_kernel(head_ref, tail_ref, mask_ref, cot_ref, head_out, tail_out, cot_out):
    edge, channels = head_ref.shape[0], head_ref.shape[1]
    low = low_half(channels)
    for pair in range(edge // 2):
        one, two = 2 * pair, 2 * pair + 1
        first = head_ref[one].astype(F32) * mask_ref[one : one + 1, :LANES].astype(F32)
        second = head_ref[two].astype(F32) * mask_ref[two : two + 1, :LANES].astype(F32)
        head_out[pair] = jnp.where(low, first, swap_halves(second)).astype(BF16)
        first = tail_ref[one].astype(F32) * mask_ref[edge + one : edge + one + 1, -LANES:].astype(F32)
        second = tail_ref[two].astype(F32) * mask_ref[edge + two : edge + two + 1, -LANES:].astype(F32)
        tail_out[pair] = jnp.where(low, swap_halves(first), second).astype(BF16)
    for peer in range(cot_out.shape[0]):
        pair = [cot_ref[2 * peer].astype(F32), cot_ref[2 * peer + 1].astype(F32)]
        cot_out[peer] = jnp.concatenate(pair, axis=1).astype(BF16)


def pick_kernel(owner_ref, returned_ref, out_ref, rank_ref):
    blocks = owner_ref.shape[0]
    low = low_half(out_ref.shape[0])
    for pair in range(blocks // 2):
        rows = []
        for side in range(2):
            block = 2 * pair + side
            owner = owner_ref[block, 0]
            rank = jnp.int32(0)
            for earlier in range(block):
                rank = rank + (owner_ref[earlier, 0] == owner).astype(jnp.int32)
            rank_ref[0, block] = owner
            rank_ref[1, block] = rank
            tile = returned_ref[owner].astype(F32)
            rows.append(jnp.where(rank == side, tile, swap_halves(tile)))
        out_ref[:, pair * LANES : (pair + 1) * LANES] = jnp.where(low, rows[0], rows[1]).astype(BF16)


def route_kernel(rank_ref, *refs):
    out_ref = refs[-1]
    blocks = rank_ref.shape[1]
    half = lax.broadcasted_iota(jnp.int32, (out_ref.shape[1], LANES), 1) // 64
    out_ref[...] = jnp.zeros_like(out_ref)
    for block in range(blocks):
        lanes = slice(block // 2 * LANES, (block // 2 + 1) * LANES)
        total = refs[0][:, lanes]
        for ref in refs[1:-1]:
            total = total + ref[:, lanes]
        owner, rank = rank_ref[0, block], rank_ref[1, block]
        tile = jnp.where(rank == block % 2, total, swap_halves(total))
        out_ref[owner] += jnp.where(half == rank, tile, 0.0).astype(BF16)


def forward_kernel(
    axis,
    nbr_ref,
    feat_ref,
    mask_ref,
    prev_ref,
    next_ref,
    wconv_ref,
    edge_ref,
    shift_ref,
    spread_ref,
    octant_ref,
    pre_out,
    octs_out,
    patches_out,
    planes,
    weights,
    own_s,
    hidden_s,
    same_from,
    same_code,
    side_from,
    side_code,
):
    blocks, channels = feat_ref.shape[0], feat_ref.shape[1]
    edge = blocks // 2
    width = wconv_ref.shape[1]
    me = lax.axis_index(axis)
    own_rows = pl.ds(pl.multiple_of(me * width, width), width)
    low = low_half(channels)
    halo = 10 * blocks
    dummy = 11 * blocks

    same, side = jnp.int32(0), jnp.int32(0)
    for block in range(blocks):
        for column in range(26):
            position = column + (column >= 13)
            source = nbr_ref[block, column]
            there = (source >= 0).astype(jnp.int32)
            step, table = position // 9, position % 9
            if step == 1:
                same_from[same] = source
                same_code[same] = block * 16 + table
                same = same + there
            else:
                side_from[side] = source
                side_code[side] = (block * 10 + (9 if step else 0)) * 32 + table * 2 + step // 2
                side = side + there

    def two_planes(first, tile):
        planes[first] = jnp.where(low, tile, 0.0).astype(BF16)
        planes[first + 1] = jnp.where(low, swap_halves(tile), 0.0).astype(BF16)

    zero_plane = jnp.zeros((channels, LANES), BF16)
    planes[dummy] = zero_plane
    for block in range(blocks):
        keep = mask_ref[block : block + 1, :].astype(F32)
        masked = feat_ref[block].astype(F32) * keep
        planes[10 * block] = zero_plane
        planes[10 * block + 9] = zero_plane
        for pair in range(4):
            two_planes(10 * block + 1 + 2 * pair, masked[:, pair * LANES : (pair + 1) * LANES])
    for pair in range(edge // 2):
        two_planes(halo + 2 * pair, prev_ref[pair].astype(F32))
        two_planes(halo + edge + 2 * pair, next_ref[pair].astype(F32))

    def same_layer(item, carry):
        code = same_code[item]
        block = lax.shift_right_logical(code, 4)
        table = edge_ref[code & 15]
        cells = planes[pl.ds(same_from[item] * 10 + 1, 8)].reshape(8 * channels, LANES)
        moved = jnp.dot(cells, table, preferred_element_type=F32).astype(BF16)
        planes[pl.ds(block * 10 + 1, 8)] += moved.reshape(8, channels, LANES)
        return carry

    lax.fori_loop(0, same, same_layer, 0)
    for extra in range(3):
        side_from[side + extra] = dummy - halo + blocks
        side_code[side + extra] = dummy * 32 + 18

    def side_layer(item, carry):
        results = []
        for extra in range(4):
            source, code = side_from[4 * item + extra], side_code[4 * item + extra]
            own = source * 10 + jnp.where(code & 1 == 1, 1, 8)
            cells = planes[jnp.where(source < blocks, own, halo + source - blocks)]
            table = edge_ref[lax.shift_right_logical(code, 1) & 15]
            moved = jnp.dot(cells, table, preferred_element_type=F32).astype(BF16)
            results.append((lax.shift_right_logical(code, 5), moved))
        for place, moved in results:
            planes[place] += moved
        return carry

    lax.fori_loop(0, lax.shift_right_logical(side + 3, 2), side_layer, 0)

    for k in range(27):
        weights[(k // 3) * width : (k // 3 + 1) * width, (k % 3) * channels : (k % 3 + 1) * channels] = wconv_ref[k]

    for block in range(0, blocks, 2):
        for plane in range(0, 10, 2):
            first, second = block * 10 + plane, block * 10 + 10 + plane
            source = jnp.concatenate(
                [
                    jnp.concatenate([planes[first], planes[first + 1]], axis=1),
                    jnp.concatenate([planes[second], planes[second + 1]], axis=1),
                ],
                axis=0,
            )
            window = lax.dot_general(shift_ref[...], source, NT, preferred_element_type=F32).astype(BF16)
            for j in range(3):
                for half in range(2):
                    row = (block + half) * STRIDE + plane * PLANE
                    patches_out[row : row + 2 * PLANE, j * channels : (j + 1) * channels] = window[
                        j * 2 * PLANE : (j + 1) * 2 * PLANE, half * channels : (half + 1) * channels
                    ]
    for block in range(blocks):
        row = block * STRIDE + 10 * PLANE
        patches_out[row : (block + 1) * STRIDE, :] = jnp.zeros((STRIDE - 10 * PLANE, 3 * channels), BF16)

    for block in range(blocks):
        own_s[block * width : (block + 1) * width, :] = feat_ref[block, own_rows, :]
    own = jnp.dot(own_s[...], spread_ref[...], preferred_element_type=F32)
    keeps = jnp.dot(mask_ref[...].astype(F32).astype(BF16), spread_ref[...], preferred_element_type=F32)
    for block in range(blocks):
        rows = slice(block * STRIDE, (block + 1) * STRIDE)
        here = slice(block * width, (block + 1) * width)
        sums = lax.dot_general(weights[...], patches_out[rows, :], NT, preferred_element_type=F32)
        keep = keeps[block : block + 1]
        pre = own[here] * keep + sums[:width, :SPAN]
        for k in range(1, 9):
            moved = pltpu.roll(sums[k * width : (k + 1) * width], STRIDE - (k // 3) * PLANE - (k % 3) * 8, 1)
            pre = pre + moved[:, :SPAN]
        pre_out[here, :] = pre
        hidden_s[here, :] = (keep * (pre * (1.0 / (1.0 + jnp.exp(-pre))))).astype(BF16)

    split_up = jnp.dot(hidden_s[...], octant_ref[...], preferred_element_type=F32)
    low = low_half(width)
    for octant in range(8):
        lanes = slice(octant * LANES, (octant + 1) * LANES)
        for pair in range(blocks // 2):
            even = split_up[2 * pair * width : (2 * pair + 1) * width, lanes]
            odd = split_up[(2 * pair + 1) * width : (2 * pair + 2) * width, lanes]
            octs_out[octant * width : (octant + 1) * width, pair * LANES : (pair + 1) * LANES] = jnp.where(
                low, even, odd
            ).astype(BF16)


def down_kernel(axes, shards, octs_ref, wdown_ref, *refs):
    dps = refs[:shards]
    pieces_out, grads_out, dp_out, spread, sums = refs[shards:]
    me = lax.axis_index(axes[1])
    core = lax.axis_index(axes[0]) & 1
    channels, total = wdown_ref.shape[2], wdown_ref.shape[1]
    width = channels // shards
    share = total // shards
    for k in range(shards):
        theirs = pl.multiple_of((me ^ k) * share, share)
        dp_out[pl.ds(theirs, share), :] = dps[k][...]
    grads = lax.dot_general(dp_out[...], octs_ref[...], NT, preferred_element_type=F32)
    sums[:, : 2 * LANES] = grads
    for k in range(shards):
        rows = pl.ds(pl.multiple_of((me ^ k) * share, share), share)
        low, high = sums[rows, :LANES], sums[rows, LANES : 2 * LANES]
        grads_out[k, core] = low
        grads_out[k, 1 - core] = high
    spread[...] = jnp.zeros_like(spread)
    for octant in range(8):
        rows = pl.ds(pl.multiple_of(octant * channels + me * width, width), width)
        spread[rows, :] = octs_ref[octant * width : (octant + 1) * width, :]
    down_weights = jnp.concatenate([wdown_ref[octant] for octant in range(8)], axis=1)
    sums[...] = jnp.dot(down_weights, spread[...], preferred_element_type=F32)
    for k in range(shards):
        pieces_out[k] = sums[pl.ds(pl.multiple_of((me ^ k) * share, share), share), :]


def backward_kernel(
    axes, dp_ref, wdown_ref, mask_ref, pre_ref, spread_ref, octant_ref, patches_ref, keep_out, give_out, dh_s, dhi, dlo, d9, conv_s
):
    blocks = mask_ref.shape[0]
    channels = wdown_ref.shape[2]
    width = pre_ref.shape[0] // blocks
    me = lax.axis_index(axes[1])
    core = lax.axis_index(axes[0]) & 1
    own_rows = pl.ds(pl.multiple_of(me * width, width), width)
    low = low_half(width)

    for octant in range(8):
        dh_s[octant] = lax.dot_general(wdown_ref[octant], dp_ref[...], TN, preferred_element_type=F32)
    for octant in range(8):
        lanes = slice(octant * LANES, (octant + 1) * LANES)
        for pair in range(blocks // 2):
            tile = dh_s[octant, own_rows, pair * LANES : (pair + 1) * LANES]
            high = tile.astype(BF16).astype(F32)
            rest = tile - high
            even = slice(2 * pair * width, (2 * pair + 1) * width)
            odd = slice((2 * pair + 1) * width, (2 * pair + 2) * width)
            dhi[even, lanes] = jnp.where(low, high, 0.0).astype(BF16)
            dhi[odd, lanes] = jnp.where(low, 0.0, high).astype(BF16)
            dlo[even, lanes] = jnp.where(low, rest, 0.0).astype(BF16)
            dlo[odd, lanes] = jnp.where(low, 0.0, rest).astype(BF16)
    dhidden = lax.dot_general(dhi[...], octant_ref[...], NT, preferred_element_type=F32)
    dhidden = dhidden + lax.dot_general(dlo[...], octant_ref[...], NT, preferred_element_type=F32)
    keeps = jnp.dot(mask_ref[...].astype(F32).astype(BF16), spread_ref[...], preferred_element_type=F32)

    blank = jnp.zeros((width, STRIDE - SPAN), F32)
    for block in range(blocks):
        rows = slice(block * width, (block + 1) * width)
        pre = pre_ref[rows, :]
        gate = 1.0 / (1.0 + jnp.exp(-pre))
        dpre = dhidden[rows] * keeps[block : block + 1] * gate * (1.0 + pre * (1.0 - gate))
        dpre = jnp.concatenate([dpre, blank], axis=1)
        lanes = slice(block * STRIDE, (block + 1) * STRIDE)
        for k in range(9):
            moved = pltpu.roll(dpre, (k // 3) * PLANE + (k % 3) * 8, 1) if k else dpre
            d9[k * width : (k + 1) * width, lanes] = moved.astype(BF16)

    for j in range(3):
        part = jnp.dot(d9[...], patches_ref[:, j * channels : (j + 1) * channels], preferred_element_type=F32)
        for k in range(9):
            at = (3 * k + j) * width
            conv_s[at : at + width] = part[k * width : (k + 1) * width]
    half = keep_out.shape[0]
    keep_out[...] = conv_s[pl.ds(pl.multiple_of(core * half, 8), half), :]
    give_out[...] = conv_s[pl.ds(pl.multiple_of((1 - core) * half, 8), half), :]


def finish_kernel(axes, shards, half, own_ref, other_ref, conv_ref, down_ref, both):
    me = lax.axis_index(axes[1])
    core = lax.axis_index(axes[0]) & 1
    share = down_ref.shape[1]
    width = LANES // shards
    both[core] = own_ref[...]
    both[1 - core] = other_ref[...]
    conv_ref[:half] = both[0, :half]
    conv_ref[half:] = both[1, :half]
    group = lax.broadcasted_iota(jnp.int32, (share, LANES), 1) // width
    for octant in range(8):
        result = jnp.zeros((share, LANES), F32)
        for k in range(shards):
            source = me ^ k
            row = half + k * share
            tile = both[octant // shards, row : row + share, :]
            turned = pltpu.roll(tile, ((source - octant % shards + shards) & (shards - 1)) * width, 1)
            result = jnp.where(group == source, turned, result)
        down_ref[octant] = result


def exchange(values, axis, step):
    count = lax.axis_size(axis)
    return lax.ppermute(values, axis, [(i, i ^ step) for i in range(count)])


def local(features, voxel_mask, neighbors, w_conv, w_down, coarse_owner, cotangent):
    blocks, channels = features.shape[0], features.shape[1]
    edge = blocks // 2
    peers = lax.axis_size("space")
    shards = lax.axis_size("chan")
    axes = ("space", "chan")
    width = w_conv.shape[1]
    total = w_down.shape[1]
    share = total // shards
    capacity = cotangent.shape[0] // peers
    lanes = blocks * 64
    tables = [jnp.asarray(t(), BF16) for t in (edge_table, shift_table, spread_table, octant_table)]
    edges, shifts, spreads, octants = tables

    head, tail, packed = pl.pallas_call(
        prepare_kernel,
        grid=(1,),
        out_shape=[
            jax.ShapeDtypeStruct((edge // 2, channels, LANES), BF16),
            jax.ShapeDtypeStruct((edge // 2, channels, LANES), BF16),
            jax.ShapeDtypeStruct((peers, share, capacity * 64), BF16),
        ],
        in_specs=[
            pl.BlockSpec((edge, channels, LANES), lambda i: (0, 0, 0)),
            pl.BlockSpec((edge, channels, LANES), lambda i: (1, 0, 3)),
            pl.BlockSpec(voxel_mask.shape, lambda i: (0, 0)),
            pl.BlockSpec(cotangent.shape, lambda i: (0, 0, 0)),
        ],
        out_specs=[
            pl.BlockSpec((edge // 2, channels, LANES), lambda i: (0, 0, 0)),
            pl.BlockSpec((edge // 2, channels, LANES), lambda i: (0, 0, 0)),
            pl.BlockSpec((peers, share, capacity * 64), lambda i: (0, 0, 0)),
        ],
    )(features, features, voxel_mask, cotangent)
    ends = peers - 1
    before = lax.ppermute(tail, "space", [(i, i + 1) for i in range(ends)])
    after = lax.ppermute(head, "space", [(i + 1, i) for i in range(ends)])
    returned = lax.all_to_all(packed, "space", split_axis=0, concat_axis=0, tiled=True)

    dpiece, place = pl.pallas_call(
        pick_kernel,
        out_shape=[
            jax.ShapeDtypeStruct((share, lanes), BF16),
            jax.ShapeDtypeStruct((2, blocks), jnp.int32),
        ],
        in_specs=[smem(), vmem()],
        out_specs=[vmem(), smem()],
    )(coarse_owner, returned)
    dpieces = [dpiece] + [exchange(dpiece, "chan", k) for k in range(1, shards)]

    pre, octs, patches = pl.pallas_call(
        functools.partial(forward_kernel, "chan"),
        out_shape=[
            jax.ShapeDtypeStruct((blocks * width, SPAN), F32),
            jax.ShapeDtypeStruct((8 * width, lanes), BF16),
            jax.ShapeDtypeStruct((blocks * STRIDE, 3 * channels), BF16),
        ],
        in_specs=[smem()] + [vmem()] * 9,
        out_specs=[vmem()] * 3,
        scratch_shapes=[
            pltpu.VMEM((11 * blocks + 1, channels, LANES), BF16),
            pltpu.VMEM((9 * width, 3 * channels), BF16),
            pltpu.VMEM((blocks * width, 512), BF16),
            pltpu.VMEM((blocks * width, SPAN), BF16),
            pltpu.SMEM((8 * blocks + 8,), jnp.int32),
            pltpu.SMEM((8 * blocks + 8,), jnp.int32),
            pltpu.SMEM((18 * blocks + 8,), jnp.int32),
            pltpu.SMEM((18 * blocks + 8,), jnp.int32),
        ],
        compiler_params=pltpu.CompilerParams(vmem_limit_bytes=40 * MIB),
    )(neighbors, features, voxel_mask, before, after, w_conv, edges, shifts, spreads, octants)

    pieces, down_grad, dp_all = pl.pallas_call(
        functools.partial(down_kernel, axes, shards),
        out_shape=[
            jax.ShapeDtypeStruct((shards, share, lanes), F32),
            jax.ShapeDtypeStruct((shards, 2, share, LANES), F32),
            jax.ShapeDtypeStruct((total, lanes), BF16),
        ],
        in_specs=[vmem()] * (2 + shards),
        out_specs=[vmem()] * 3,
        scratch_shapes=[pltpu.VMEM((8 * channels, lanes), BF16), pltpu.VMEM((total, lanes), F32)],
        compiler_params=pltpu.CompilerParams(vmem_limit_bytes=24 * MIB),
    )(octs, w_down, *dpieces)
    downs = [down_grad[0]] + [exchange(down_grad[k], "chan", k) for k in range(1, shards)]
    parts = [pieces[0]] + [exchange(pieces[k], "chan", k) for k in range(1, shards)]

    half = 27 * width // 2
    conv_keep, conv_give = pl.pallas_call(
        functools.partial(backward_kernel, axes),
        out_shape=[jax.ShapeDtypeStruct((half, channels), F32)] * 2,
        in_specs=[vmem()] * 7,
        out_specs=[vmem()] * 2,
        scratch_shapes=[
            pltpu.VMEM((8, channels, lanes), F32),
            pltpu.VMEM((blocks * width, 8 * LANES), BF16),
            pltpu.VMEM((blocks * width, 8 * LANES), BF16),
            pltpu.VMEM((9 * width, blocks * STRIDE), BF16),
            pltpu.VMEM((27 * width, channels), F32),
        ],
        compiler_params=pltpu.CompilerParams(vmem_limit_bytes=40 * MIB),
    )(dp_all, w_down, voxel_mask, pre, spreads, octants, patches)

    outgoing = pl.pallas_call(
        route_kernel,
        out_shape=jax.ShapeDtypeStruct((peers, share, capacity * 64), BF16),
        in_specs=[smem()] + [vmem()] * shards,
        out_specs=vmem(),
    )(place, *parts)
    coarse = lax.all_to_all(outgoing, "space", split_axis=0, concat_axis=0, tiled=True)
    coarse = coarse.reshape(peers, share, capacity, 64).transpose(0, 2, 1, 3).reshape(peers * capacity, share, 64)

    keep = jnp.concatenate([conv_keep] + [d[0] for d in downs])
    give = jnp.concatenate([conv_give] + [d[1] for d in downs])
    mine = keep + exchange(give, "space", 1)
    cut = mine.shape[0] // 2
    first, second = mine[:cut], mine[cut:]
    steps = []
    step = 2
    while step < peers:
        steps.append(step)
        step *= 2
    for near, far in zip(steps, reversed(steps)):
        first = first + exchange(first, "space", near)
        second = second + exchange(second, "space", far)
    mine = jnp.concatenate([first, second])
    other = exchange(mine, "space", 1)
    conv_sum, down_sum = pl.pallas_call(
        functools.partial(finish_kernel, axes, shards, half),
        out_shape=[
            jax.ShapeDtypeStruct((27 * width, channels), F32),
            jax.ShapeDtypeStruct((8, share, channels), F32),
        ],
        in_specs=[vmem(), vmem()],
        out_specs=[vmem()] * 2,
        scratch_shapes=[pltpu.VMEM((2,) + mine.shape, F32)],
    )(mine, other)
    return coarse, conv_sum.reshape(27, width, channels), down_sum


def solution(mesh):
    in_specs = (
        P("space", None, None),
        P("space", None),
        P("space", None),
        P(None, "chan", None),
        P(),
        P("space", None),
        P("space", "chan", None),
    )
    out_specs = (P("space", "chan", None), P(None, "chan", None), P(None, "chan", None))
    return jax.shard_map(local, mesh=mesh, in_specs=in_specs, out_specs=out_specs, check_vma=False)
```

```python
import functools

import jax
import jax.numpy as jnp
from jax import lax
from jax.experimental import pallas as pl
from jax.experimental.pallas import tpu as pltpu
from jax.sharding import PartitionSpec as P

F32 = jnp.float32
BF16 = jnp.bfloat16
SIGNS = (-1, 0, 1)
LANES = 128
NT = (((1,), (1,)), ((), ()))
TN = (((0,), (0,)), ((), ()))
MIB = 1024 * 1024
PLANE = 80
STRIDE = 896
SPAN = 640


def vmem():
    return pl.BlockSpec(memory_space=pltpu.VMEM)


def smem():
    return pl.BlockSpec(memory_space=pltpu.SMEM)


def cost(microseconds):
    return pl.CostEstimate(flops=int(microseconds * 1.15e9), bytes_accessed=0, transcendentals=0)


def rim_lane(cell_y, cell_z):
    high_y, high_z = (cell_y > 0).astype(jnp.int32), (cell_z > 0).astype(jnp.int32)
    own_y, own_z = (cell_y >= 0) & (cell_y < 8), (cell_z >= 0) & (cell_z < 8)
    edges = jnp.where(own_z, 64 + 8 * high_y + cell_z, 80 + 8 * high_z + cell_y)
    lane = jnp.where(own_y & own_z, 8 * cell_y + cell_z, edges)
    return jnp.where(own_y | own_z, lane, 96 + 2 * high_y + high_z)


def column(rows):
    return lax.broadcasted_iota(jnp.int32, (rows, 1), 0)


def row(lanes):
    return lax.broadcasted_iota(jnp.int32, (1, lanes), 1)


def equal(left, right):
    return jnp.where(left == right, 1.0, 0.0).astype(BF16)


def edge_table(step_y, step_z):
    source = column(LANES)
    far_y, far_z = (source >> 3) + 8 * step_y, (source & 7) + 8 * step_z
    there = (source < 64) & (far_y >= -1) & (far_y <= 8) & (far_z >= -1) & (far_z <= 8)
    return equal(jnp.where(there, rim_lane(far_y, far_z), -1), row(LANES))


def shift_table(step_z):
    cell = column(2 * PLANE)
    plane = (cell >= PLANE).astype(jnp.int32)
    cell = cell - plane * PLANE
    lane = rim_lane((cell >> 3) - 1, (cell & 7) + step_z)
    return equal(plane * LANES + lane, row(2 * LANES))


def spread_table():
    voxel = column(512)
    return equal((voxel >> 6) * PLANE + (voxel & 63), row(SPAN))


def octant_table(plane):
    cell = column(PLANE)
    octant = 4 * (plane % 2) + 2 * ((cell >> 3) & 1) + (cell & 1)
    place = 16 * (plane // 2) + 4 * ((cell >> 4) & 3) + ((cell >> 1) & 3)
    lane = row(8 * LANES)
    return equal(jnp.where(cell < 64, octant * 64 + place, -1), (lane >> 7) * 64 + (lane & 63))


def low_half(rows):
    return lax.broadcasted_iota(jnp.int32, (rows, LANES), 1) < 64


def swap_halves(tile):
    return pltpu.roll(tile, 64, 1)


def prepare_kernel(head_ref, tail_ref, mask_ref, cot_ref, head_out, tail_out, cot_out):
    edge, channels = head_ref.shape[0], head_ref.shape[1]
    low = low_half(channels)
    for pair in range(edge // 2):
        one, two = 2 * pair, 2 * pair + 1
        first = head_ref[one].astype(F32) * mask_ref[one : one + 1, :LANES].astype(F32)
        second = head_ref[two].astype(F32) * mask_ref[two : two + 1, :LANES].astype(F32)
        head_out[pair] = jnp.where(low, first, swap_halves(second)).astype(BF16)
        first = tail_ref[one].astype(F32) * mask_ref[edge + one : edge + one + 1, -LANES:].astype(F32)
        second = tail_ref[two].astype(F32) * mask_ref[edge + two : edge + two + 1, -LANES:].astype(F32)
        tail_out[pair] = jnp.where(low, swap_halves(first), second).astype(BF16)
    for peer in range(cot_out.shape[0]):
        pair = [cot_ref[2 * peer].astype(F32), cot_ref[2 * peer + 1].astype(F32)]
        cot_out[peer] = jnp.concatenate(pair, axis=1).astype(BF16)


def pick_kernel(owner_ref, returned_ref, out_ref, rank_ref):
    blocks = owner_ref.shape[1]
    low = low_half(out_ref.shape[0])
    for pair in range(blocks // 2):
        rows = []
        for side in range(2):
            block = 2 * pair + side
            owner = owner_ref[0, block]
            rank = jnp.int32(0)
            for earlier in range(block):
                rank = rank + (owner_ref[0, earlier] == owner).astype(jnp.int32)
            rank_ref[0, block] = owner
            rank_ref[1, block] = rank
            tile = returned_ref[owner].astype(F32)
            rows.append(jnp.where(rank == side, tile, swap_halves(tile)))
        out_ref[:, pair * LANES : (pair + 1) * LANES] = jnp.where(low, rows[0], rows[1]).astype(BF16)


def route_kernel(rank_ref, *refs):
    out_ref = refs[-1]
    blocks = rank_ref.shape[1]
    half = lax.broadcasted_iota(jnp.int32, (out_ref.shape[1], LANES), 1) // 64
    out_ref[...] = jnp.zeros_like(out_ref)
    for block in range(blocks):
        lanes = slice(block // 2 * LANES, (block // 2 + 1) * LANES)
        total = refs[0][:, lanes]
        for ref in refs[1:-1]:
            total = total + ref[:, lanes]
        owner, rank = rank_ref[0, block], rank_ref[1, block]
        tile = jnp.where(rank == block % 2, total, swap_halves(total))
        out_ref[owner] += jnp.where(half == rank, tile, 0.0).astype(BF16)


def forward_kernel(
    axis,
    prev_ref,
    next_ref,
    nbr_hbm,
    feat_hbm,
    mask_hbm,
    wconv_hbm,
    pre_out,
    octs_out,
    patches_out,
    spread_ref,
    octant_ref,
    planes,
    weights,
    own_s,
    hidden_s,
    same_from,
    same_code,
    side_from,
    side_code,
    nbr_ref,
    feat_ref,
    mask_ref,
    wconv_ref,
    edge_ref,
    shift_ref,
    sems,
):
    loads = [
        pltpu.make_async_copy(source, target, sems.at[i])
        for i, (source, target) in enumerate(
            [
                (nbr_hbm, nbr_ref),
                (mask_hbm, mask_ref),
                (feat_hbm, feat_ref),
                (wconv_hbm, wconv_ref),
            ]
        )
    ]
    for load in loads:
        load.start()
    blocks, channels = feat_ref.shape[0], feat_ref.shape[1]
    edge = blocks // 2
    width = wconv_ref.shape[1]
    me = lax.axis_index(axis)
    own_rows = pl.ds(pl.multiple_of(me * width, width), width)
    low = low_half(channels)
    halo = 10 * blocks
    dummy = 11 * blocks

    for table in range(9):
        edge_ref[table] = edge_table(table // 3 - 1, table % 3 - 1)
    edge_ref[9] = jnp.zeros((LANES, LANES), BF16)
    for j in range(3):
        shift_ref[j * 2 * PLANE : (j + 1) * 2 * PLANE, :] = shift_table(j - 1)
    spread_ref[...] = spread_table()
    for plane in range(8):
        octant_ref[plane * PLANE : (plane + 1) * PLANE, :] = octant_table(plane)

    loads[0].wait()
    same, side = jnp.int32(0), jnp.int32(0)
    for block in range(blocks):
        for column in range(26):
            position = column + (column >= 13)
            source = nbr_ref[block, column]
            there = (source >= 0).astype(jnp.int32)
            step, table = position // 9, position % 9
            if step == 1:
                same_from[same] = source
                same_code[same] = block * 16 + table
                same = same + there
            else:
                side_from[side] = source
                side_code[side] = (block * 10 + (9 if step else 0)) * 32 + table * 2 + step // 2
                side = side + there

    loads[1].wait()
    loads[2].wait()
    def two_planes(first, tile):
        planes[first] = jnp.where(low, tile, 0.0).astype(BF16)
        planes[first + 1] = jnp.where(low, swap_halves(tile), 0.0).astype(BF16)

    zero_plane = jnp.zeros((channels, LANES), BF16)
    planes[dummy] = zero_plane
    for block in range(blocks):
        keep = mask_ref[block : block + 1, :].astype(F32)
        masked = feat_ref[block].astype(F32) * keep
        planes[10 * block] = zero_plane
        planes[10 * block + 9] = zero_plane
        for pair in range(4):
            two_planes(10 * block + 1 + 2 * pair, masked[:, pair * LANES : (pair + 1) * LANES])
    for pair in range(edge // 2):
        two_planes(halo + 2 * pair, prev_ref[pair].astype(F32))
        two_planes(halo + edge + 2 * pair, next_ref[pair].astype(F32))

    def same_layer(item, carry):
        code = same_code[item]
        block = lax.shift_right_logical(code, 4)
        table = edge_ref[code & 15]
        cells = planes[pl.ds(same_from[item] * 10 + 1, 8)].reshape(8 * channels, LANES)
        moved = jnp.dot(cells, table, preferred_element_type=F32).astype(BF16)
        planes[pl.ds(block * 10 + 1, 8)] += moved.reshape(8, channels, LANES)
        return carry

    lax.fori_loop(0, same, same_layer, 0)
    for extra in range(3):
        side_from[side + extra] = dummy - halo + blocks
        side_code[side + extra] = dummy * 32 + 18

    def side_layer(item, carry):
        results = []
        for extra in range(4):
            source, code = side_from[4 * item + extra], side_code[4 * item + extra]
            own = source * 10 + jnp.where(code & 1 == 1, 1, 8)
            cells = planes[jnp.where(source < blocks, own, halo + source - blocks)]
            table = edge_ref[lax.shift_right_logical(code, 1) & 15]
            moved = jnp.dot(cells, table, preferred_element_type=F32).astype(BF16)
            results.append((lax.shift_right_logical(code, 5), moved))
        for place, moved in results:
            planes[place] += moved
        return carry

    lax.fori_loop(0, lax.shift_right_logical(side + 3, 2), side_layer, 0)

    loads[3].wait()
    for k in range(27):
        weights[(k // 3) * width : (k // 3 + 1) * width, (k % 3) * channels : (k % 3 + 1) * channels] = wconv_ref[k]

    for block in range(0, blocks, 2):
        for plane in range(0, 10, 2):
            first, second = block * 10 + plane, block * 10 + 10 + plane
            source = jnp.concatenate(
                [
                    jnp.concatenate([planes[first], planes[first + 1]], axis=1),
                    jnp.concatenate([planes[second], planes[second + 1]], axis=1),
                ],
                axis=0,
            )
            window = lax.dot_general(shift_ref[...], source, NT, preferred_element_type=F32).astype(BF16)
            for j in range(3):
                for half in range(2):
                    row = (block + half) * STRIDE + plane * PLANE
                    patches_out[row : row + 2 * PLANE, j * channels : (j + 1) * channels] = window[
                        j * 2 * PLANE : (j + 1) * 2 * PLANE, half * channels : (half + 1) * channels
                    ]
    for block in range(blocks):
        row = block * STRIDE + 10 * PLANE
        patches_out[row : (block + 1) * STRIDE, :] = jnp.zeros((STRIDE - 10 * PLANE, 3 * channels), BF16)

    for block in range(blocks):
        own_s[block * width : (block + 1) * width, :] = feat_ref[block, own_rows, :]
    own = jnp.dot(own_s[...], spread_ref[...], preferred_element_type=F32)
    keeps = jnp.dot(mask_ref[...].astype(F32).astype(BF16), spread_ref[...], preferred_element_type=F32)
    for block in range(blocks):
        rows = slice(block * STRIDE, (block + 1) * STRIDE)
        here = slice(block * width, (block + 1) * width)
        sums = lax.dot_general(weights[...], patches_out[rows, :], NT, preferred_element_type=F32)
        keep = keeps[block : block + 1]
        pre = own[here] * keep + sums[:width, :SPAN]
        for k in range(1, 9):
            moved = pltpu.roll(sums[k * width : (k + 1) * width], STRIDE - (k // 3) * PLANE - (k % 3) * 8, 1)
            pre = pre + moved[:, :SPAN]
        pre_out[here, :] = pre
        hidden_s[here, :] = (keep * (pre * (1.0 / (1.0 + jnp.exp(-pre))))).astype(BF16)

    split_up = jnp.dot(hidden_s[...], octant_ref[...], preferred_element_type=F32)
    low = low_half(width)
    for octant in range(8):
        lanes = slice(octant * LANES, (octant + 1) * LANES)
        for pair in range(blocks // 2):
            even = split_up[2 * pair * width : (2 * pair + 1) * width, lanes]
            odd = split_up[(2 * pair + 1) * width : (2 * pair + 2) * width, lanes]
            octs_out[octant * width : (octant + 1) * width, pair * LANES : (pair + 1) * LANES] = jnp.where(
                low, even, odd
            ).astype(BF16)


def down_kernel(axes, shards, octs_ref, wdown_ref, *refs):
    dps = refs[:shards]
    pieces_out, grads_out, dp_out, spread, sums = refs[shards:]
    me = lax.axis_index(axes[1])
    core = lax.axis_index(axes[0]) & 1
    channels, total = wdown_ref.shape[2], wdown_ref.shape[1]
    width = channels // shards
    share = total // shards
    for k in range(shards):
        theirs = pl.multiple_of((me ^ k) * share, share)
        dp_out[pl.ds(theirs, share), :] = dps[k][...]
    grads = lax.dot_general(dp_out[...], octs_ref[...], NT, preferred_element_type=F32)
    sums[:, : 2 * LANES] = grads
    for k in range(shards):
        rows = pl.ds(pl.multiple_of((me ^ k) * share, share), share)
        low, high = sums[rows, :LANES], sums[rows, LANES : 2 * LANES]
        grads_out[k, core] = low
        grads_out[k, 1 - core] = high
    spread[...] = jnp.zeros_like(spread)
    for octant in range(8):
        rows = pl.ds(pl.multiple_of(octant * channels + me * width, width), width)
        spread[rows, :] = octs_ref[octant * width : (octant + 1) * width, :]
    down_weights = jnp.concatenate([wdown_ref[octant] for octant in range(8)], axis=1)
    sums[...] = jnp.dot(down_weights, spread[...], preferred_element_type=F32)
    for k in range(shards):
        pieces_out[k] = sums[pl.ds(pl.multiple_of((me ^ k) * share, share), share), :]


def backward_kernel(
    axes, dp_ref, wdown_ref, mask_ref, pre_ref, spread_ref, octant_ref, patches_ref, keep_out, give_out, dh_s, dhi, dlo, d9, conv_s
):
    blocks = mask_ref.shape[0]
    channels = wdown_ref.shape[2]
    width = pre_ref.shape[0] // blocks
    me = lax.axis_index(axes[1])
    core = lax.axis_index(axes[0]) & 1
    own_rows = pl.ds(pl.multiple_of(me * width, width), width)
    low = low_half(width)

    for octant in range(8):
        dh_s[octant] = lax.dot_general(wdown_ref[octant], dp_ref[...], TN, preferred_element_type=F32)
    for octant in range(8):
        lanes = slice(octant * LANES, (octant + 1) * LANES)
        for pair in range(blocks // 2):
            tile = dh_s[octant, own_rows, pair * LANES : (pair + 1) * LANES]
            high = tile.astype(BF16).astype(F32)
            rest = tile - high
            even = slice(2 * pair * width, (2 * pair + 1) * width)
            odd = slice((2 * pair + 1) * width, (2 * pair + 2) * width)
            dhi[even, lanes] = jnp.where(low, high, 0.0).astype(BF16)
            dhi[odd, lanes] = jnp.where(low, 0.0, high).astype(BF16)
            dlo[even, lanes] = jnp.where(low, rest, 0.0).astype(BF16)
            dlo[odd, lanes] = jnp.where(low, 0.0, rest).astype(BF16)
    dhidden = lax.dot_general(dhi[...], octant_ref[...], NT, preferred_element_type=F32)
    dhidden = dhidden + lax.dot_general(dlo[...], octant_ref[...], NT, preferred_element_type=F32)
    keeps = jnp.dot(mask_ref[...].astype(F32).astype(BF16), spread_ref[...], preferred_element_type=F32)

    blank = jnp.zeros((width, STRIDE - SPAN), F32)
    for block in range(blocks):
        rows = slice(block * width, (block + 1) * width)
        pre = pre_ref[rows, :]
        gate = 1.0 / (1.0 + jnp.exp(-pre))
        dpre = dhidden[rows] * keeps[block : block + 1] * gate * (1.0 + pre * (1.0 - gate))
        dpre = jnp.concatenate([dpre, blank], axis=1)
        lanes = slice(block * STRIDE, (block + 1) * STRIDE)
        for k in range(9):
            moved = pltpu.roll(dpre, (k // 3) * PLANE + (k % 3) * 8, 1) if k else dpre
            d9[k * width : (k + 1) * width, lanes] = moved.astype(BF16)

    for j in range(3):
        part = jnp.dot(d9[...], patches_ref[:, j * channels : (j + 1) * channels], preferred_element_type=F32)
        for k in range(9):
            at = (3 * k + j) * width
            conv_s[at : at + width] = part[k * width : (k + 1) * width]
    half = keep_out.shape[0]
    keep_out[...] = conv_s[pl.ds(pl.multiple_of(core * half, 8), half), :]
    give_out[...] = conv_s[pl.ds(pl.multiple_of((1 - core) * half, 8), half), :]


def finish_kernel(axes, shards, half, own_ref, other_ref, conv_ref, down_ref, both):
    me = lax.axis_index(axes[1])
    core = lax.axis_index(axes[0]) & 1
    share = down_ref.shape[1]
    width = LANES // shards
    both[core] = own_ref[...]
    both[1 - core] = other_ref[...]
    conv_ref[:half] = both[0, :half]
    conv_ref[half:] = both[1, :half]
    group = lax.broadcasted_iota(jnp.int32, (share, LANES), 1) // width
    for octant in range(8):
        result = jnp.zeros((share, LANES), F32)
        for k in range(shards):
            source = me ^ k
            row = half + k * share
            tile = both[octant // shards, row : row + share, :]
            turned = pltpu.roll(tile, ((source - octant % shards + shards) & (shards - 1)) * width, 1)
            result = jnp.where(group == source, turned, result)
        down_ref[octant] = result


def exchange(values, axis, step):
    count = lax.axis_size(axis)
    return lax.ppermute(values, axis, [(i, i ^ step) for i in range(count)])


def local(features, voxel_mask, neighbors, w_conv, w_down, coarse_owner, cotangent):
    blocks, channels = features.shape[0], features.shape[1]
    edge = blocks // 2
    peers = lax.axis_size("space")
    shards = lax.axis_size("chan")
    axes = ("space", "chan")
    width = w_conv.shape[1]
    total = w_down.shape[1]
    share = total // shards
    capacity = cotangent.shape[0] // peers
    lanes = blocks * 64

    head, tail, packed = pl.pallas_call(
        prepare_kernel,
        grid=(1,),
        out_shape=[
            jax.ShapeDtypeStruct((edge // 2, channels, LANES), BF16),
            jax.ShapeDtypeStruct((edge // 2, channels, LANES), BF16),
            jax.ShapeDtypeStruct((peers, share, capacity * 64), BF16),
        ],
        in_specs=[
            pl.BlockSpec((edge, channels, LANES), lambda i: (0, 0, 0)),
            pl.BlockSpec((edge, channels, LANES), lambda i: (1, 0, 3)),
            pl.BlockSpec(voxel_mask.shape, lambda i: (0, 0)),
            pl.BlockSpec(cotangent.shape, lambda i: (0, 0, 0)),
        ],
        out_specs=[
            pl.BlockSpec((edge // 2, channels, LANES), lambda i: (0, 0, 0)),
            pl.BlockSpec((edge // 2, channels, LANES), lambda i: (0, 0, 0)),
            pl.BlockSpec((peers, share, capacity * 64), lambda i: (0, 0, 0)),
        ],
        cost_estimate=cost(2),
        compiler_params=pltpu.CompilerParams(vmem_limit_bytes=60 * MIB),
    )(features, features, voxel_mask, cotangent)
    ends = peers - 1
    before = lax.ppermute(tail, "space", [(i, i + 1) for i in range(ends)])
    after = lax.ppermute(head, "space", [(i + 1, i) for i in range(ends)])
    returned = lax.all_to_all(packed, "space", split_axis=0, concat_axis=0, tiled=True)

    dpiece, place = pl.pallas_call(
        pick_kernel,
        out_shape=[
            jax.ShapeDtypeStruct((share, lanes), BF16),
            jax.ShapeDtypeStruct((2, blocks), jnp.int32),
        ],
        in_specs=[smem(), vmem()],
        out_specs=[vmem(), smem()],
        cost_estimate=cost(1.5),
        compiler_params=pltpu.CompilerParams(vmem_limit_bytes=8 * MIB),
    )(coarse_owner.reshape(1, blocks), returned)
    dpieces = [dpiece] + [exchange(dpiece, "chan", k) for k in range(1, shards)]

    pre, octs, patches, spreads, octants = pl.pallas_call(
        functools.partial(forward_kernel, "chan"),
        out_shape=[
            jax.ShapeDtypeStruct((blocks * width, SPAN), F32),
            jax.ShapeDtypeStruct((8 * width, lanes), BF16),
            jax.ShapeDtypeStruct((blocks * STRIDE, 3 * channels), BF16),
            jax.ShapeDtypeStruct((512, SPAN), BF16),
            jax.ShapeDtypeStruct((SPAN, 8 * LANES), BF16),
        ],
        in_specs=[vmem()] * 2 + [pl.BlockSpec(memory_space=pltpu.HBM)] * 4,
        out_specs=[vmem()] * 5,
        scratch_shapes=[
            pltpu.VMEM((11 * blocks + 1, channels, LANES), BF16),
            pltpu.VMEM((9 * width, 3 * channels), BF16),
            pltpu.VMEM((blocks * width, 512), BF16),
            pltpu.VMEM((blocks * width, SPAN), BF16),
            pltpu.SMEM((8 * blocks + 8,), jnp.int32),
            pltpu.SMEM((8 * blocks + 8,), jnp.int32),
            pltpu.SMEM((18 * blocks + 8,), jnp.int32),
            pltpu.SMEM((18 * blocks + 8,), jnp.int32),
            pltpu.SMEM(neighbors.shape, jnp.int32),
            pltpu.VMEM(features.shape, BF16),
            pltpu.VMEM(voxel_mask.shape, jnp.int32),
            pltpu.VMEM(w_conv.shape, BF16),
            pltpu.VMEM((10, LANES, LANES), BF16),
            pltpu.VMEM((3 * 2 * PLANE, 2 * LANES), BF16),
            pltpu.SemaphoreType.DMA((4,)),
        ],
        cost_estimate=cost(8),
        compiler_params=pltpu.CompilerParams(vmem_limit_bytes=40 * MIB),
    )(before, after, neighbors, features, voxel_mask, w_conv)

    pieces, down_grad, dp_all = pl.pallas_call(
        functools.partial(down_kernel, axes, shards),
        out_shape=[
            jax.ShapeDtypeStruct((shards, share, lanes), F32),
            jax.ShapeDtypeStruct((shards, 2, share, LANES), F32),
            jax.ShapeDtypeStruct((total, lanes), BF16),
        ],
        in_specs=[vmem()] * (2 + shards),
        out_specs=[vmem()] * 3,
        scratch_shapes=[pltpu.VMEM((8 * channels, lanes), BF16), pltpu.VMEM((total, lanes), F32)],
        cost_estimate=cost(1),
        compiler_params=pltpu.CompilerParams(vmem_limit_bytes=24 * MIB),
    )(octs, w_down, *dpieces)
    downs = [down_grad[0]] + [exchange(down_grad[k], "chan", k) for k in range(1, shards)]
    parts = [pieces[0]] + [exchange(pieces[k], "chan", k) for k in range(1, shards)]

    half = 27 * width // 2
    conv_keep, conv_give = pl.pallas_call(
        functools.partial(backward_kernel, axes),
        out_shape=[jax.ShapeDtypeStruct((half, channels), F32)] * 2,
        in_specs=[vmem()] * 7,
        out_specs=[vmem()] * 2,
        scratch_shapes=[
            pltpu.VMEM((8, channels, lanes), F32),
            pltpu.VMEM((blocks * width, 8 * LANES), BF16),
            pltpu.VMEM((blocks * width, 8 * LANES), BF16),
            pltpu.VMEM((9 * width, blocks * STRIDE), BF16),
            pltpu.VMEM((27 * width, channels), F32),
        ],
        cost_estimate=cost(6),
        compiler_params=pltpu.CompilerParams(vmem_limit_bytes=40 * MIB),
    )(dp_all, w_down, voxel_mask, pre, spreads, octants, patches)

    outgoing = pl.pallas_call(
        route_kernel,
        out_shape=jax.ShapeDtypeStruct((peers, share, capacity * 64), BF16),
        in_specs=[smem()] + [vmem()] * shards,
        out_specs=vmem(),
        cost_estimate=cost(1.5),
        compiler_params=pltpu.CompilerParams(vmem_limit_bytes=8 * MIB),
    )(place, *parts)
    coarse = lax.all_to_all(outgoing, "space", split_axis=0, concat_axis=0, tiled=True)
    coarse = coarse.reshape(peers, share, capacity, 64).transpose(0, 2, 1, 3).reshape(peers * capacity, share, 64)

    keep = jnp.concatenate([conv_keep] + [d[0] for d in downs])
    give = jnp.concatenate([conv_give] + [d[1] for d in downs])
    mine = keep + exchange(give, "space", 1)
    cut = mine.shape[0] // 2
    first, second = mine[:cut], mine[cut:]
    steps = []
    step = 2
    while step < peers:
        steps.append(step)
        step *= 2
    for near, far in zip(steps, reversed(steps)):
        first = first + exchange(first, "space", near)
        second = second + exchange(second, "space", far)
    mine = jnp.concatenate([first, second])
    other = exchange(mine, "space", 1)
    conv_sum, down_sum = pl.pallas_call(
        functools.partial(finish_kernel, axes, shards, half),
        out_shape=[
            jax.ShapeDtypeStruct((27 * width, channels), F32),
            jax.ShapeDtypeStruct((8, share, channels), F32),
        ],
        in_specs=[vmem(), vmem()],
        out_specs=[vmem()] * 2,
        scratch_shapes=[pltpu.VMEM((2,) + mine.shape, F32)],
        cost_estimate=cost(1.5),
        compiler_params=pltpu.CompilerParams(vmem_limit_bytes=8 * MIB),
    )(mine, other)
    return coarse, conv_sum.reshape(27, width, channels), down_sum


def solution(mesh):
    in_specs = (
        P("space", None, None),
        P("space", None),
        P("space", None),
        P(None, "chan", None),
        P(),
        P("space", None),
        P("space", "chan", None),
    )
    out_specs = (P("space", "chan", None), P(None, "chan", None), P(None, "chan", None))
    return jax.shard_map(local, mesh=mesh, in_specs=in_specs, out_specs=out_specs, check_vma=False)
```

```python
import functools

import jax
import jax.numpy as jnp
from jax import lax
from jax.experimental import pallas as pl
from jax.experimental.pallas import tpu as pltpu
from jax.sharding import PartitionSpec as P

F32 = jnp.float32
BF16 = jnp.bfloat16
SIGNS = (-1, 0, 1)
LANES = 128
NT = (((1,), (1,)), ((), ()))
TN = (((0,), (0,)), ((), ()))
MIB = 1024 * 1024
PLANE = 80
STRIDE = 896
SPAN = 640


def vmem():
    return pl.BlockSpec(memory_space=pltpu.VMEM)


def smem():
    return pl.BlockSpec(memory_space=pltpu.SMEM)


def cost(microseconds):
    return pl.CostEstimate(flops=int(microseconds * 1.15e9), bytes_accessed=0, transcendentals=0)


def rim_lane(cell_y, cell_z):
    high_y, high_z = (cell_y > 0).astype(jnp.int32), (cell_z > 0).astype(jnp.int32)
    own_y, own_z = (cell_y >= 0) & (cell_y < 8), (cell_z >= 0) & (cell_z < 8)
    edges = jnp.where(own_z, 64 + 8 * high_y + cell_z, 80 + 8 * high_z + cell_y)
    lane = jnp.where(own_y & own_z, 8 * cell_y + cell_z, edges)
    return jnp.where(own_y | own_z, lane, 96 + 2 * high_y + high_z)


def column(rows):
    return lax.broadcasted_iota(jnp.int32, (rows, 1), 0)


def row(lanes):
    return lax.broadcasted_iota(jnp.int32, (1, lanes), 1)


def equal(left, right):
    return jnp.where(left == right, 1.0, 0.0).astype(BF16)


def edge_table(step_y, step_z):
    source = column(LANES)
    far_y, far_z = (source >> 3) + 8 * step_y, (source & 7) + 8 * step_z
    there = (source < 64) & (far_y >= -1) & (far_y <= 8) & (far_z >= -1) & (far_z <= 8)
    return equal(jnp.where(there, rim_lane(far_y, far_z), -1), row(LANES))


def shift_table(step_z):
    cell = column(2 * PLANE)
    plane = (cell >= PLANE).astype(jnp.int32)
    cell = cell - plane * PLANE
    lane = rim_lane((cell >> 3) - 1, (cell & 7) + step_z)
    return equal(plane * LANES + lane, row(2 * LANES))


def spread_table():
    voxel = column(512)
    return equal((voxel >> 6) * PLANE + (voxel & 63), row(SPAN))


def octant_table(plane):
    cell = column(PLANE)
    octant = 4 * (plane % 2) + 2 * ((cell >> 3) & 1) + (cell & 1)
    place = 16 * (plane // 2) + 4 * ((cell >> 4) & 3) + ((cell >> 1) & 3)
    lane = row(8 * LANES)
    return equal(jnp.where(cell < 64, octant * 64 + place, -1), (lane >> 7) * 64 + (lane & 63))


def low_half(rows):
    return lax.broadcasted_iota(jnp.int32, (rows, LANES), 1) < 64


def swap_halves(tile):
    return pltpu.roll(tile, 64, 1)


def prepare_kernel(head_ref, tail_ref, mask_ref, cot_ref, head_out, tail_out, cot_out):
    edge, channels = head_ref.shape[0], head_ref.shape[1]
    low = low_half(channels)
    for pair in range(edge // 2):
        one, two = 2 * pair, 2 * pair + 1
        first = head_ref[one].astype(F32) * mask_ref[one : one + 1, :LANES].astype(F32)
        second = head_ref[two].astype(F32) * mask_ref[two : two + 1, :LANES].astype(F32)
        head_out[pair] = jnp.where(low, first, swap_halves(second)).astype(BF16)
        first = tail_ref[one].astype(F32) * mask_ref[edge + one : edge + one + 1, -LANES:].astype(F32)
        second = tail_ref[two].astype(F32) * mask_ref[edge + two : edge + two + 1, -LANES:].astype(F32)
        tail_out[pair] = jnp.where(low, swap_halves(first), second).astype(BF16)
    for peer in range(cot_out.shape[0]):
        pair = [cot_ref[2 * peer].astype(F32), cot_ref[2 * peer + 1].astype(F32)]
        cot_out[peer] = jnp.concatenate(pair, axis=1).astype(BF16)


def pick_kernel(owner_ref, returned_ref, out_ref, rank_ref):
    blocks = owner_ref.shape[1]
    low = low_half(out_ref.shape[0])
    for pair in range(blocks // 2):
        rows = []
        for side in range(2):
            block = 2 * pair + side
            owner = owner_ref[0, block]
            rank = jnp.int32(0)
            for earlier in range(block):
                rank = rank + (owner_ref[0, earlier] == owner).astype(jnp.int32)
            rank_ref[0, block] = owner
            rank_ref[1, block] = rank
            tile = returned_ref[owner].astype(F32)
            rows.append(jnp.where(rank == side, tile, swap_halves(tile)))
        out_ref[:, pair * LANES : (pair + 1) * LANES] = jnp.where(low, rows[0], rows[1]).astype(BF16)


def route_kernel(rank_ref, *refs):
    out_ref = refs[-1]
    blocks = rank_ref.shape[1]
    half = lax.broadcasted_iota(jnp.int32, (out_ref.shape[1], LANES), 1) // 64
    out_ref[...] = jnp.zeros_like(out_ref)
    for block in range(blocks):
        lanes = slice(block // 2 * LANES, (block // 2 + 1) * LANES)
        total = refs[0][:, lanes]
        for ref in refs[1:-1]:
            total = total + ref[:, lanes]
        owner, rank = rank_ref[0, block], rank_ref[1, block]
        tile = jnp.where(rank == block % 2, total, swap_halves(total))
        out_ref[owner] += jnp.where(half == rank, tile, 0.0).astype(BF16)


def forward_kernel(
    axis,
    prev_ref,
    next_ref,
    nbr_hbm,
    feat_hbm,
    mask_hbm,
    wconv_hbm,
    pre_out,
    octs_out,
    patches_out,
    spread_ref,
    octant_ref,
    planes,
    weights,
    own_s,
    hidden_s,
    same_from,
    same_code,
    side_from,
    side_code,
    nbr_ref,
    feat_ref,
    mask_ref,
    wconv_ref,
    edge_ref,
    shift_ref,
    sems,
):
    loads = [
        pltpu.make_async_copy(source, target, sems.at[i])
        for i, (source, target) in enumerate(
            [
                (nbr_hbm, nbr_ref),
                (mask_hbm, mask_ref),
                (feat_hbm, feat_ref),
                (wconv_hbm, wconv_ref),
            ]
        )
    ]
    for load in loads:
        load.start()
    blocks, channels = feat_ref.shape[0], feat_ref.shape[1]
    edge = blocks // 2
    width = wconv_ref.shape[1]
    me = lax.axis_index(axis)
    own_rows = pl.ds(pl.multiple_of(me * width, width), width)
    low = low_half(channels)
    halo = 10 * blocks
    dummy = 11 * blocks

    for table in range(9):
        edge_ref[table] = edge_table(table // 3 - 1, table % 3 - 1)
    edge_ref[9] = jnp.zeros((LANES, LANES), BF16)
    for j in range(3):
        shift_ref[j * 2 * PLANE : (j + 1) * 2 * PLANE, :] = shift_table(j - 1)
    spread_ref[...] = spread_table()
    for plane in range(8):
        octant_ref[plane * PLANE : (plane + 1) * PLANE, :] = octant_table(plane)

    loads[0].wait()
    same, side = jnp.int32(0), jnp.int32(0)
    for block in range(blocks):
        for column in range(26):
            position = column + (column >= 13)
            source = nbr_ref[block, column]
            there = (source >= 0).astype(jnp.int32)
            step, table = position // 9, position % 9
            if step == 1:
                same_from[same] = source
                same_code[same] = block * 16 + table
                same = same + there
            else:
                side_from[side] = source
                side_code[side] = (block * 10 + (9 if step else 0)) * 32 + table * 2 + step // 2
                side = side + there

    loads[1].wait()
    loads[2].wait()
    def two_planes(first, tile):
        planes[first] = jnp.where(low, tile, 0.0).astype(BF16)
        planes[first + 1] = jnp.where(low, swap_halves(tile), 0.0).astype(BF16)

    zero_plane = jnp.zeros((channels, LANES), BF16)
    planes[dummy] = zero_plane
    for block in range(blocks):
        keep = mask_ref[block : block + 1, :].astype(F32)
        masked = feat_ref[block].astype(F32) * keep
        planes[10 * block] = zero_plane
        planes[10 * block + 9] = zero_plane
        for pair in range(4):
            two_planes(10 * block + 1 + 2 * pair, masked[:, pair * LANES : (pair + 1) * LANES])
    for pair in range(edge // 2):
        two_planes(halo + 2 * pair, prev_ref[pair].astype(F32))
        two_planes(halo + edge + 2 * pair, next_ref[pair].astype(F32))

    same_from[same] = 0
    same_code[same] = 9

    def same_layer(item, carry):
        results = []
        for extra in range(2):
            code = same_code[2 * item + extra]
            cells = planes[pl.ds(same_from[2 * item + extra] * 10 + 1, 8)].reshape(8 * channels, LANES)
            moved = jnp.dot(cells, edge_ref[code & 15], preferred_element_type=F32).astype(BF16)
            results.append((lax.shift_right_logical(code, 4), moved.reshape(8, channels, LANES)))
        for block, moved in results:
            planes[pl.ds(block * 10 + 1, 8)] += moved
        return carry

    lax.fori_loop(0, lax.shift_right_logical(same + 1, 1), same_layer, 0)
    for extra in range(3):
        side_from[side + extra] = dummy - halo + blocks
        side_code[side + extra] = dummy * 32 + 18

    def side_layer(item, carry):
        results = []
        for extra in range(4):
            source, code = side_from[4 * item + extra], side_code[4 * item + extra]
            own = source * 10 + jnp.where(code & 1 == 1, 1, 8)
            cells = planes[jnp.where(source < blocks, own, halo + source - blocks)]
            table = edge_ref[lax.shift_right_logical(code, 1) & 15]
            moved = jnp.dot(cells, table, preferred_element_type=F32).astype(BF16)
            results.append((lax.shift_right_logical(code, 5), moved))
        for place, moved in results:
            planes[place] += moved
        return carry

    lax.fori_loop(0, lax.shift_right_logical(side + 3, 2), side_layer, 0)

    loads[3].wait()
    for k in range(27):
        weights[(k // 3) * width : (k // 3 + 1) * width, (k % 3) * channels : (k % 3 + 1) * channels] = wconv_ref[k]

    for block in range(0, blocks, 2):
        for plane in range(0, 10, 2):
            first, second = block * 10 + plane, block * 10 + 10 + plane
            source = jnp.concatenate(
                [
                    jnp.concatenate([planes[first], planes[first + 1]], axis=1),
                    jnp.concatenate([planes[second], planes[second + 1]], axis=1),
                ],
                axis=0,
            )
            window = lax.dot_general(shift_ref[...], source, NT, preferred_element_type=F32).astype(BF16)
            for j in range(3):
                for half in range(2):
                    row = (block + half) * STRIDE + plane * PLANE
                    patches_out[row : row + 2 * PLANE, j * channels : (j + 1) * channels] = window[
                        j * 2 * PLANE : (j + 1) * 2 * PLANE, half * channels : (half + 1) * channels
                    ]
    for block in range(blocks):
        row = block * STRIDE + 10 * PLANE
        patches_out[row : (block + 1) * STRIDE, :] = jnp.zeros((STRIDE - 10 * PLANE, 3 * channels), BF16)

    for block in range(blocks):
        own_s[block * width : (block + 1) * width, :] = feat_ref[block, own_rows, :]
    own = jnp.dot(own_s[...], spread_ref[...], preferred_element_type=F32)
    keeps = jnp.dot(mask_ref[...].astype(F32).astype(BF16), spread_ref[...], preferred_element_type=F32)
    for block in range(blocks):
        rows = slice(block * STRIDE, (block + 1) * STRIDE)
        here = slice(block * width, (block + 1) * width)
        sums = lax.dot_general(weights[...], patches_out[rows, :], NT, preferred_element_type=F32)
        keep = keeps[block : block + 1]
        pre = own[here] * keep + sums[:width, :SPAN]
        for k in range(1, 9):
            moved = pltpu.roll(sums[k * width : (k + 1) * width], STRIDE - (k // 3) * PLANE - (k % 3) * 8, 1)
            pre = pre + moved[:, :SPAN]
        pre_out[here, :] = pre
        hidden_s[here, :] = (keep * (pre * (1.0 / (1.0 + jnp.exp(-pre))))).astype(BF16)

    split_up = jnp.dot(hidden_s[...], octant_ref[...], preferred_element_type=F32)
    low = low_half(width)
    for octant in range(8):
        lanes = slice(octant * LANES, (octant + 1) * LANES)
        for pair in range(blocks // 2):
            even = split_up[2 * pair * width : (2 * pair + 1) * width, lanes]
            odd = split_up[(2 * pair + 1) * width : (2 * pair + 2) * width, lanes]
            octs_out[octant * width : (octant + 1) * width, pair * LANES : (pair + 1) * LANES] = jnp.where(
                low, even, odd
            ).astype(BF16)


def down_kernel(axes, shards, octs_ref, wdown_ref, *refs):
    dps = refs[:shards]
    pieces_out, grads_out, dp_out, spread, sums = refs[shards:]
    me = lax.axis_index(axes[1])
    core = lax.axis_index(axes[0]) & 1
    channels, total = wdown_ref.shape[2], wdown_ref.shape[1]
    width = channels // shards
    share = total // shards
    for k in range(shards):
        theirs = pl.multiple_of((me ^ k) * share, share)
        dp_out[pl.ds(theirs, share), :] = dps[k][...]
    grads = lax.dot_general(dp_out[...], octs_ref[...], NT, preferred_element_type=F32)
    sums[:, : 2 * LANES] = grads
    for k in range(shards):
        rows = pl.ds(pl.multiple_of((me ^ k) * share, share), share)
        low, high = sums[rows, :LANES], sums[rows, LANES : 2 * LANES]
        grads_out[k, core] = low
        grads_out[k, 1 - core] = high
    spread[...] = jnp.zeros_like(spread)
    for octant in range(8):
        rows = pl.ds(pl.multiple_of(octant * channels + me * width, width), width)
        spread[rows, :] = octs_ref[octant * width : (octant + 1) * width, :]
    down_weights = jnp.concatenate([wdown_ref[octant] for octant in range(8)], axis=1)
    sums[...] = jnp.dot(down_weights, spread[...], preferred_element_type=F32)
    for k in range(shards):
        pieces_out[k] = sums[pl.ds(pl.multiple_of((me ^ k) * share, share), share), :]


def backward_kernel(
    axes, dp_ref, wdown_ref, mask_ref, pre_ref, spread_ref, octant_ref, patches_ref, keep_out, give_out, dh_s, dhi, dlo, d9, conv_s
):
    blocks = mask_ref.shape[0]
    channels = wdown_ref.shape[2]
    width = pre_ref.shape[0] // blocks
    me = lax.axis_index(axes[1])
    core = lax.axis_index(axes[0]) & 1
    own_rows = pl.ds(pl.multiple_of(me * width, width), width)
    low = low_half(width)

    for octant in range(8):
        dh_s[octant] = lax.dot_general(wdown_ref[octant], dp_ref[...], TN, preferred_element_type=F32)
    for octant in range(8):
        lanes = slice(octant * LANES, (octant + 1) * LANES)
        for pair in range(blocks // 2):
            tile = dh_s[octant, own_rows, pair * LANES : (pair + 1) * LANES]
            high = tile.astype(BF16).astype(F32)
            rest = tile - high
            even = slice(2 * pair * width, (2 * pair + 1) * width)
            odd = slice((2 * pair + 1) * width, (2 * pair + 2) * width)
            dhi[even, lanes] = jnp.where(low, high, 0.0).astype(BF16)
            dhi[odd, lanes] = jnp.where(low, 0.0, high).astype(BF16)
            dlo[even, lanes] = jnp.where(low, rest, 0.0).astype(BF16)
            dlo[odd, lanes] = jnp.where(low, 0.0, rest).astype(BF16)
    dhidden = lax.dot_general(dhi[...], octant_ref[...], NT, preferred_element_type=F32)
    dhidden = dhidden + lax.dot_general(dlo[...], octant_ref[...], NT, preferred_element_type=F32)
    keeps = jnp.dot(mask_ref[...].astype(F32).astype(BF16), spread_ref[...], preferred_element_type=F32)

    blank = jnp.zeros((width, STRIDE - SPAN), F32)
    for block in range(blocks):
        rows = slice(block * width, (block + 1) * width)
        pre = pre_ref[rows, :]
        gate = 1.0 / (1.0 + jnp.exp(-pre))
        dpre = dhidden[rows] * keeps[block : block + 1] * gate * (1.0 + pre * (1.0 - gate))
        dpre = jnp.concatenate([dpre, blank], axis=1)
        lanes = slice(block * STRIDE, (block + 1) * STRIDE)
        for k in range(9):
            moved = pltpu.roll(dpre, (k // 3) * PLANE + (k % 3) * 8, 1) if k else dpre
            d9[k * width : (k + 1) * width, lanes] = moved.astype(BF16)

    part = jnp.dot(d9[...], patches_ref[...], preferred_element_type=F32)
    for k in range(27):
        conv_s[k * width : (k + 1) * width] = part[
            k // 3 * width : (k // 3 + 1) * width, k % 3 * channels : (k % 3 + 1) * channels
        ]
    half = keep_out.shape[0]
    keep_out[...] = conv_s[pl.ds(pl.multiple_of(core * half, 8), half), :]
    give_out[...] = conv_s[pl.ds(pl.multiple_of((1 - core) * half, 8), half), :]


def finish_kernel(axes, shards, half, own_ref, other_ref, conv_ref, down_ref, both):
    me = lax.axis_index(axes[1])
    core = lax.axis_index(axes[0]) & 1
    share = down_ref.shape[1]
    width = LANES // shards
    both[core] = own_ref[...]
    both[1 - core] = other_ref[...]
    conv_ref[:half] = both[0, :half]
    conv_ref[half:] = both[1, :half]
    group = lax.broadcasted_iota(jnp.int32, (share, LANES), 1) // width
    for octant in range(8):
        result = jnp.zeros((share, LANES), F32)
        for k in range(shards):
            source = me ^ k
            row = half + k * share
            tile = both[octant // shards, row : row + share, :]
            turned = pltpu.roll(tile, ((source - octant % shards + shards) & (shards - 1)) * width, 1)
            result = jnp.where(group == source, turned, result)
        down_ref[octant] = result


def exchange(values, axis, step):
    count = lax.axis_size(axis)
    return lax.ppermute(values, axis, [(i, i ^ step) for i in range(count)])


def local(features, voxel_mask, neighbors, w_conv, w_down, coarse_owner, cotangent):
    blocks, channels = features.shape[0], features.shape[1]
    edge = blocks // 2
    peers = lax.axis_size("space")
    shards = lax.axis_size("chan")
    axes = ("space", "chan")
    width = w_conv.shape[1]
    total = w_down.shape[1]
    share = total // shards
    capacity = cotangent.shape[0] // peers
    lanes = blocks * 64

    head, tail, packed = pl.pallas_call(
        prepare_kernel,
        grid=(1,),
        out_shape=[
            jax.ShapeDtypeStruct((edge // 2, channels, LANES), BF16),
            jax.ShapeDtypeStruct((edge // 2, channels, LANES), BF16),
            jax.ShapeDtypeStruct((peers, share, capacity * 64), BF16),
        ],
        in_specs=[
            pl.BlockSpec((edge, channels, LANES), lambda i: (0, 0, 0)),
            pl.BlockSpec((edge, channels, LANES), lambda i: (1, 0, 3)),
            pl.BlockSpec(voxel_mask.shape, lambda i: (0, 0)),
            pl.BlockSpec(cotangent.shape, lambda i: (0, 0, 0)),
        ],
        out_specs=[
            pl.BlockSpec((edge // 2, channels, LANES), lambda i: (0, 0, 0)),
            pl.BlockSpec((edge // 2, channels, LANES), lambda i: (0, 0, 0)),
            pl.BlockSpec((peers, share, capacity * 64), lambda i: (0, 0, 0)),
        ],
        cost_estimate=cost(2),
        compiler_params=pltpu.CompilerParams(vmem_limit_bytes=60 * MIB),
    )(features, features, voxel_mask, cotangent)
    ends = peers - 1
    before = lax.ppermute(tail, "space", [(i, i + 1) for i in range(ends)])
    after = lax.ppermute(head, "space", [(i + 1, i) for i in range(ends)])
    returned = lax.all_to_all(packed, "space", split_axis=0, concat_axis=0, tiled=True)

    dpiece, place = pl.pallas_call(
        pick_kernel,
        out_shape=[
            jax.ShapeDtypeStruct((share, lanes), BF16),
            jax.ShapeDtypeStruct((2, blocks), jnp.int32),
        ],
        in_specs=[smem(), vmem()],
        out_specs=[vmem(), smem()],
        cost_estimate=cost(1.5),
        compiler_params=pltpu.CompilerParams(vmem_limit_bytes=8 * MIB),
    )(coarse_owner.reshape(1, blocks), returned)
    dpieces = [dpiece] + [exchange(dpiece, "chan", k) for k in range(1, shards)]

    pre, octs, patches, spreads, octants = pl.pallas_call(
        functools.partial(forward_kernel, "chan"),
        out_shape=[
            jax.ShapeDtypeStruct((blocks * width, SPAN), F32),
            jax.ShapeDtypeStruct((8 * width, lanes), BF16),
            jax.ShapeDtypeStruct((blocks * STRIDE, 3 * channels), BF16),
            jax.ShapeDtypeStruct((512, SPAN), BF16),
            jax.ShapeDtypeStruct((SPAN, 8 * LANES), BF16),
        ],
        in_specs=[vmem()] * 2 + [pl.BlockSpec(memory_space=pltpu.HBM)] * 4,
        out_specs=[vmem()] * 5,
        scratch_shapes=[
            pltpu.VMEM((11 * blocks + 1, channels, LANES), BF16),
            pltpu.VMEM((9 * width, 3 * channels), BF16),
            pltpu.VMEM((blocks * width, 512), BF16),
            pltpu.VMEM((blocks * width, SPAN), BF16),
            pltpu.SMEM((8 * blocks + 8,), jnp.int32),
            pltpu.SMEM((8 * blocks + 8,), jnp.int32),
            pltpu.SMEM((18 * blocks + 8,), jnp.int32),
            pltpu.SMEM((18 * blocks + 8,), jnp.int32),
            pltpu.SMEM(neighbors.shape, jnp.int32),
            pltpu.VMEM(features.shape, BF16),
            pltpu.VMEM(voxel_mask.shape, jnp.int32),
            pltpu.VMEM(w_conv.shape, BF16),
            pltpu.VMEM((10, LANES, LANES), BF16),
            pltpu.VMEM((3 * 2 * PLANE, 2 * LANES), BF16),
            pltpu.SemaphoreType.DMA((4,)),
        ],
        cost_estimate=cost(8),
        compiler_params=pltpu.CompilerParams(vmem_limit_bytes=40 * MIB),
    )(before, after, neighbors, features, voxel_mask, w_conv)

    pieces, down_grad, dp_all = pl.pallas_call(
        functools.partial(down_kernel, axes, shards),
        out_shape=[
            jax.ShapeDtypeStruct((shards, share, lanes), F32),
            jax.ShapeDtypeStruct((shards, 2, share, LANES), F32),
            jax.ShapeDtypeStruct((total, lanes), BF16),
        ],
        in_specs=[vmem()] * (2 + shards),
        out_specs=[vmem()] * 3,
        scratch_shapes=[pltpu.VMEM((8 * channels, lanes), BF16), pltpu.VMEM((total, lanes), F32)],
        cost_estimate=cost(1),
        compiler_params=pltpu.CompilerParams(vmem_limit_bytes=24 * MIB),
    )(octs, w_down, *dpieces)
    downs = [down_grad[0]] + [exchange(down_grad[k], "chan", k) for k in range(1, shards)]
    parts = [pieces[0]] + [exchange(pieces[k], "chan", k) for k in range(1, shards)]

    half = 27 * width // 2
    conv_keep, conv_give = pl.pallas_call(
        functools.partial(backward_kernel, axes),
        out_shape=[jax.ShapeDtypeStruct((half, channels), F32)] * 2,
        in_specs=[vmem()] * 7,
        out_specs=[vmem()] * 2,
        scratch_shapes=[
            pltpu.VMEM((8, channels, lanes), F32),
            pltpu.VMEM((blocks * width, 8 * LANES), BF16),
            pltpu.VMEM((blocks * width, 8 * LANES), BF16),
            pltpu.VMEM((9 * width, blocks * STRIDE), BF16),
            pltpu.VMEM((27 * width, channels), F32),
        ],
        cost_estimate=cost(6),
        compiler_params=pltpu.CompilerParams(vmem_limit_bytes=40 * MIB),
    )(dp_all, w_down, voxel_mask, pre, spreads, octants, patches)

    outgoing = pl.pallas_call(
        route_kernel,
        out_shape=jax.ShapeDtypeStruct((peers, share, capacity * 64), BF16),
        in_specs=[smem()] + [vmem()] * shards,
        out_specs=vmem(),
        cost_estimate=cost(1.5),
        compiler_params=pltpu.CompilerParams(vmem_limit_bytes=8 * MIB),
    )(place, *parts)
    coarse = lax.all_to_all(outgoing, "space", split_axis=0, concat_axis=0, tiled=True)
    coarse = coarse.reshape(peers, share, capacity, 64).transpose(0, 2, 1, 3).reshape(peers * capacity, share, 64)

    keep = jnp.concatenate([conv_keep] + [d[0] for d in downs])
    give = jnp.concatenate([conv_give] + [d[1] for d in downs])
    mine = keep + exchange(give, "space", 1)
    step = 2
    while step < peers:
        mine = mine + exchange(mine, "space", step)
        step *= 2
    other = exchange(mine, "space", 1)
    conv_sum, down_sum = pl.pallas_call(
        functools.partial(finish_kernel, axes, shards, half),
        out_shape=[
            jax.ShapeDtypeStruct((27 * width, channels), F32),
            jax.ShapeDtypeStruct((8, share, channels), F32),
        ],
        in_specs=[vmem(), vmem()],
        out_specs=[vmem()] * 2,
        scratch_shapes=[pltpu.VMEM((2,) + mine.shape, F32)],
        cost_estimate=cost(1.5),
        compiler_params=pltpu.CompilerParams(vmem_limit_bytes=8 * MIB),
    )(mine, other)
    return coarse, conv_sum.reshape(27, width, channels), down_sum


def solution(mesh):
    in_specs = (
        P("space", None, None),
        P("space", None),
        P("space", None),
        P(None, "chan", None),
        P(),
        P("space", None),
        P("space", "chan", None),
    )
    out_specs = (P("space", "chan", None), P(None, "chan", None), P(None, "chan", None))
    return jax.shard_map(local, mesh=mesh, in_specs=in_specs, out_specs=out_specs, check_vma=False)
```

```python
import functools

import jax
import jax.numpy as jnp
from jax import lax
from jax.experimental import pallas as pl
from jax.experimental.pallas import tpu as pltpu
from jax.sharding import PartitionSpec as P

F32 = jnp.float32
BF16 = jnp.bfloat16
SIGNS = (-1, 0, 1)
LANES = 128
NT = (((1,), (1,)), ((), ()))
TN = (((0,), (0,)), ((), ()))
MIB = 1024 * 1024
PLANE = 80
STRIDE = 896
SPAN = 640


def vmem():
    return pl.BlockSpec(memory_space=pltpu.VMEM)


def cost(microseconds):
    return pl.CostEstimate(flops=int(microseconds * 1.15e9), bytes_accessed=0, transcendentals=0)


def rim_lane(cell_y, cell_z):
    high_y, high_z = (cell_y > 0).astype(jnp.int32), (cell_z > 0).astype(jnp.int32)
    own_y, own_z = (cell_y >= 0) & (cell_y < 8), (cell_z >= 0) & (cell_z < 8)
    edges = jnp.where(own_z, 64 + 8 * high_y + cell_z, 80 + 8 * high_z + cell_y)
    lane = jnp.where(own_y & own_z, 8 * cell_y + cell_z, edges)
    return jnp.where(own_y | own_z, lane, 96 + 2 * high_y + high_z)


def column(rows):
    return lax.broadcasted_iota(jnp.int32, (rows, 1), 0)


def row(lanes):
    return lax.broadcasted_iota(jnp.int32, (1, lanes), 1)


def equal(left, right):
    return jnp.where(left == right, 1.0, 0.0).astype(BF16)


def edge_table(step_y, step_z):
    source = column(LANES)
    far_y, far_z = (source >> 3) + 8 * step_y, (source & 7) + 8 * step_z
    there = (source < 64) & (far_y >= -1) & (far_y <= 8) & (far_z >= -1) & (far_z <= 8)
    return equal(jnp.where(there, rim_lane(far_y, far_z), -1), row(LANES))


def shift_table(step_z):
    cell = column(2 * PLANE)
    plane = (cell >= PLANE).astype(jnp.int32)
    cell = cell - plane * PLANE
    lane = rim_lane((cell >> 3) - 1, (cell & 7) + step_z)
    return equal(plane * LANES + lane, row(2 * LANES))


def spread_table():
    voxel = column(512)
    return equal((voxel >> 6) * PLANE + (voxel & 63), row(SPAN))


def octant_table(plane):
    cell = column(PLANE)
    octant = 4 * (plane % 2) + 2 * ((cell >> 3) & 1) + (cell & 1)
    place = 16 * (plane // 2) + 4 * ((cell >> 4) & 3) + ((cell >> 1) & 3)
    return equal(jnp.where(cell < 64, octant * 64 + place, -1), row(8 * 64))


def low_half(rows):
    return lax.broadcasted_iota(jnp.int32, (rows, LANES), 1) < 64


def swap_halves(tile):
    return pltpu.roll(tile, 64, 1)


def prepare_kernel(head_ref, tail_ref, mask_ref, cot_ref, head_out, tail_out, cot_out):
    edge, channels = head_ref.shape[0], head_ref.shape[1]
    low = low_half(channels)
    for pair in range(edge // 2):
        one, two = 2 * pair, 2 * pair + 1
        first = head_ref[one].astype(F32) * mask_ref[one : one + 1, :LANES].astype(F32)
        second = head_ref[two].astype(F32) * mask_ref[two : two + 1, :LANES].astype(F32)
        head_out[pair] = jnp.where(low, first, swap_halves(second)).astype(BF16)
        first = tail_ref[one].astype(F32) * mask_ref[edge + one : edge + one + 1, -LANES:].astype(F32)
        second = tail_ref[two].astype(F32) * mask_ref[edge + two : edge + two + 1, -LANES:].astype(F32)
        tail_out[pair] = jnp.where(low, swap_halves(first), second).astype(BF16)
    for peer in range(cot_out.shape[0]):
        pair = [cot_ref[2 * peer].astype(F32), cot_ref[2 * peer + 1].astype(F32)]
        cot_out[peer] = jnp.concatenate(pair, axis=1).astype(BF16)


def pick_kernel(owner_ref, returned_ref, out_ref, slot_ref):
    blocks = owner_ref.shape[1]
    share = out_ref.shape[0]
    low = low_half(share)
    owners = owner_ref[...].astype(F32)
    block = lax.broadcasted_iota(jnp.int32, (blocks, blocks), 0)
    other = lax.broadcasted_iota(jnp.int32, (blocks, blocks), 1)
    owner = jnp.sum(jnp.where(block == other, owners, 0.0), axis=1, keepdims=True)
    rank = jnp.sum(jnp.where((owner == owners) & (other < block), 1.0, 0.0), axis=1, keepdims=True)
    slots = jnp.broadcast_to((2.0 * owner + rank).astype(jnp.int32), (blocks, LANES))
    slot_ref[...] = slots
    sources = [returned_ref[peer].astype(F32) for peer in range(returned_ref.shape[0])]
    for pair in range(blocks // 2):
        tiles = []
        for side in range(2):
            slot = jnp.broadcast_to(slots[2 * pair + side : 2 * pair + side + 1], (share, LANES))
            tile = sources[0]
            for peer in range(1, len(sources)):
                tile = jnp.where((slot >> 1) == peer, sources[peer], tile)
            tiles.append(jnp.where((slot & 1) == side, tile, swap_halves(tile)))
        out_ref[:, pair * LANES : (pair + 1) * LANES] = jnp.where(low, tiles[0], tiles[1]).astype(BF16)


def route_kernel(slot_ref, *refs):
    out_ref = refs[-1]
    blocks, share = slot_ref.shape[0], out_ref.shape[1]
    half = lax.broadcasted_iota(jnp.int32, (share, LANES), 1) // 64
    pieces = []
    for block in range(blocks):
        lanes = slice(block // 2 * LANES, (block // 2 + 1) * LANES)
        total = refs[0][:, lanes]
        for ref in refs[1:-1]:
            total = total + ref[:, lanes]
        slot = jnp.broadcast_to(slot_ref[block : block + 1, :], (share, LANES))
        rank = slot & 1
        tile = jnp.where(rank == block % 2, total, swap_halves(total))
        pieces.append((jnp.where(half == rank, slot >> 1, -1), tile))
    for peer in range(out_ref.shape[0]):
        tile = jnp.zeros((share, LANES), F32)
        for owner, piece in pieces:
            tile = jnp.where(owner == peer, piece, tile)
        out_ref[peer] = tile.astype(BF16)


def forward_kernel(
    axis,
    prev_ref,
    next_ref,
    nbr_hbm,
    feat_hbm,
    mask_hbm,
    wconv_hbm,
    pre_out,
    octs_out,
    patches_out,
    spread_ref,
    octant_ref,
    planes,
    weights,
    own_s,
    hidden_s,
    same_from,
    same_code,
    side_from,
    side_code,
    nbr_ref,
    feat_ref,
    mask_ref,
    wconv_ref,
    edge_ref,
    shift_ref,
    sems,
):
    loads = [
        pltpu.make_async_copy(source, target, sems.at[i])
        for i, (source, target) in enumerate(
            [
                (nbr_hbm, nbr_ref),
                (mask_hbm, mask_ref),
                (feat_hbm, feat_ref),
                (wconv_hbm, wconv_ref),
            ]
        )
    ]
    for load in loads:
        load.start()
    blocks, channels = feat_ref.shape[0], feat_ref.shape[1]
    edge = blocks // 2
    width = wconv_ref.shape[1]
    me = lax.axis_index(axis)
    own_rows = pl.ds(pl.multiple_of(me * width, width), width)
    low = low_half(channels)
    halo = 10 * blocks
    dummy = 11 * blocks

    for table in range(9):
        edge_ref[table] = edge_table(table // 3 - 1, table % 3 - 1)
    edge_ref[9] = jnp.zeros((LANES, LANES), BF16)
    for j in range(3):
        shift_ref[j * 2 * PLANE : (j + 1) * 2 * PLANE, :] = shift_table(j - 1)
    spread_ref[...] = spread_table()
    for plane in range(8):
        octant_ref[plane * PLANE : (plane + 1) * PLANE, :] = octant_table(plane)

    loads[0].wait()
    same, side = jnp.int32(0), jnp.int32(0)
    for block in range(blocks):
        for column in range(26):
            position = column + (column >= 13)
            source = nbr_ref[block, column]
            there = (source >= 0).astype(jnp.int32)
            step, table = position // 9, position % 9
            if step == 1:
                same_from[same] = source
                same_code[same] = block * 16 + table
                same = same + there
            else:
                side_from[side] = source
                side_code[side] = (block * 10 + (9 if step else 0)) * 32 + table * 2 + step // 2
                side = side + there

    loads[1].wait()
    loads[2].wait()
    def two_planes(first, tile):
        planes[first] = jnp.where(low, tile, 0.0).astype(BF16)
        planes[first + 1] = jnp.where(low, swap_halves(tile), 0.0).astype(BF16)

    zero_plane = jnp.zeros((channels, LANES), BF16)
    planes[dummy] = zero_plane
    for block in range(blocks):
        keep = mask_ref[block : block + 1, :].astype(F32)
        masked = feat_ref[block].astype(F32) * keep
        planes[10 * block] = zero_plane
        planes[10 * block + 9] = zero_plane
        for pair in range(4):
            two_planes(10 * block + 1 + 2 * pair, masked[:, pair * LANES : (pair + 1) * LANES])
    for pair in range(edge // 2):
        two_planes(halo + 2 * pair, prev_ref[pair].astype(F32))
        two_planes(halo + edge + 2 * pair, next_ref[pair].astype(F32))

    same_from[same] = 0
    same_code[same] = 9

    def same_layer(item, carry):
        results = []
        for extra in range(2):
            code = same_code[2 * item + extra]
            cells = planes[pl.ds(same_from[2 * item + extra] * 10 + 1, 8)].reshape(8 * channels, LANES)
            moved = jnp.dot(cells, edge_ref[code & 15], preferred_element_type=F32).astype(BF16)
            results.append((lax.shift_right_logical(code, 4), moved.reshape(8, channels, LANES)))
        for block, moved in results:
            planes[pl.ds(block * 10 + 1, 8)] += moved
        return carry

    lax.fori_loop(0, lax.shift_right_logical(same + 1, 1), same_layer, 0)
    for extra in range(3):
        side_from[side + extra] = dummy - halo + blocks
        side_code[side + extra] = dummy * 32 + 18

    def side_layer(item, carry):
        results = []
        for extra in range(4):
            source, code = side_from[4 * item + extra], side_code[4 * item + extra]
            own = source * 10 + jnp.where(code & 1 == 1, 1, 8)
            cells = planes[jnp.where(source < blocks, own, halo + source - blocks)]
            table = edge_ref[lax.shift_right_logical(code, 1) & 15]
            moved = jnp.dot(cells, table, preferred_element_type=F32).astype(BF16)
            results.append((lax.shift_right_logical(code, 5), moved))
        for place, moved in results:
            planes[place] += moved
        return carry

    lax.fori_loop(0, lax.shift_right_logical(side + 3, 2), side_layer, 0)

    loads[3].wait()
    for k in range(27):
        weights[(k // 3) * width : (k // 3 + 1) * width, (k % 3) * channels : (k % 3 + 1) * channels] = wconv_ref[k]

    for block in range(0, blocks, 2):
        for plane in range(0, 10, 2):
            first, second = block * 10 + plane, block * 10 + 10 + plane
            source = jnp.concatenate(
                [
                    jnp.concatenate([planes[first], planes[first + 1]], axis=1),
                    jnp.concatenate([planes[second], planes[second + 1]], axis=1),
                ],
                axis=0,
            )
            window = lax.dot_general(shift_ref[...], source, NT, preferred_element_type=F32).astype(BF16)
            for j in range(3):
                for half in range(2):
                    row = (block + half) * STRIDE + plane * PLANE
                    patches_out[row : row + 2 * PLANE, j * channels : (j + 1) * channels] = window[
                        j * 2 * PLANE : (j + 1) * 2 * PLANE, half * channels : (half + 1) * channels
                    ]
    for block in range(blocks):
        row = block * STRIDE + 10 * PLANE
        patches_out[row : (block + 1) * STRIDE, :] = jnp.zeros((STRIDE - 10 * PLANE, 3 * channels), BF16)

    for block in range(blocks):
        own_s[block * width : (block + 1) * width, :] = feat_ref[block, own_rows, :]
    own = jnp.dot(own_s[...], spread_ref[...], preferred_element_type=F32)
    keeps = jnp.dot(mask_ref[...].astype(F32).astype(BF16), spread_ref[...], preferred_element_type=F32)
    for block in range(blocks):
        rows = slice(block * STRIDE, (block + 1) * STRIDE)
        here = slice(block * width, (block + 1) * width)
        sums = lax.dot_general(weights[...], patches_out[rows, :], NT, preferred_element_type=F32)
        keep = keeps[block : block + 1]
        pre = own[here] * keep + sums[:width, :SPAN]
        for k in range(1, 9):
            moved = pltpu.roll(sums[k * width : (k + 1) * width], STRIDE - (k // 3) * PLANE - (k % 3) * 8, 1)
            pre = pre + moved[:, :SPAN]
        pre_out[here, :] = pre
        hidden_s[here, :] = (keep * (pre * (1.0 / (1.0 + jnp.exp(-pre))))).astype(BF16)

    split_up = jnp.dot(hidden_s[...], octant_ref[...], preferred_element_type=F32)
    low = low_half(width)
    for octant in range(0, 8, 2):
        lanes = slice(octant * 64, octant * 64 + LANES)
        for pair in range(blocks // 2):
            even = split_up[2 * pair * width : (2 * pair + 1) * width, lanes]
            odd = split_up[(2 * pair + 1) * width : (2 * pair + 2) * width, lanes]
            at = slice(pair * LANES, (pair + 1) * LANES)
            first = jnp.where(low, even, swap_halves(odd)).astype(BF16)
            second = jnp.where(low, swap_halves(even), odd).astype(BF16)
            octs_out[octant * width : (octant + 1) * width, at] = first
            octs_out[(octant + 1) * width : (octant + 2) * width, at] = second


def down_kernel(axes, shards, octs_ref, wdown_ref, *refs):
    dps = refs[:shards]
    pieces_out, grads_out, dp_out, spread, sums = refs[shards:]
    me = lax.axis_index(axes[1])
    core = lax.axis_index(axes[0]) & 1
    channels, total = wdown_ref.shape[2], wdown_ref.shape[1]
    width = channels // shards
    share = total // shards
    for k in range(shards):
        theirs = pl.multiple_of((me ^ k) * share, share)
        dp_out[pl.ds(theirs, share), :] = dps[k][...]
    grads = lax.dot_general(dp_out[...], octs_ref[...], NT, preferred_element_type=F32)
    sums[:, : 2 * LANES] = grads
    for k in range(shards):
        rows = pl.ds(pl.multiple_of((me ^ k) * share, share), share)
        low, high = sums[rows, :LANES], sums[rows, LANES : 2 * LANES]
        grads_out[k, core] = low
        grads_out[k, 1 - core] = high
    spread[...] = jnp.zeros_like(spread)
    for octant in range(8):
        rows = pl.ds(pl.multiple_of(octant * channels + me * width, width), width)
        spread[rows, :] = octs_ref[octant * width : (octant + 1) * width, :]
    down_weights = jnp.concatenate([wdown_ref[octant] for octant in range(8)], axis=1)
    sums[...] = jnp.dot(down_weights, spread[...], preferred_element_type=F32)
    for k in range(shards):
        pieces_out[k] = sums[pl.ds(pl.multiple_of((me ^ k) * share, share), share), :]


def backward_kernel(
    axes, dp_ref, wdown_ref, mask_ref, pre_ref, spread_ref, octant_ref, patches_ref, keep_out, give_out, dh_s, dhi, dlo, d9, conv_s
):
    blocks = mask_ref.shape[0]
    channels = wdown_ref.shape[2]
    width = pre_ref.shape[0] // blocks
    me = lax.axis_index(axes[1])
    core = lax.axis_index(axes[0]) & 1
    own_rows = pl.ds(pl.multiple_of(me * width, width), width)
    low = low_half(width)

    for octant in range(8):
        dh_s[octant] = lax.dot_general(wdown_ref[octant], dp_ref[...], TN, preferred_element_type=F32)
    for octant in range(0, 8, 2):
        lanes = slice(octant * 64, octant * 64 + LANES)
        for pair in range(blocks // 2):
            at = slice(pair * LANES, (pair + 1) * LANES)
            first, second = dh_s[octant, own_rows, at], dh_s[octant + 1, own_rows, at]
            for block, tile in (
                (2 * pair, jnp.where(low, first, swap_halves(second))),
                (2 * pair + 1, jnp.where(low, swap_halves(first), second)),
            ):
                rows = slice(block * width, (block + 1) * width)
                high = tile.astype(BF16)
                dhi[rows, lanes] = high
                dlo[rows, lanes] = (tile - high.astype(F32)).astype(BF16)
    dhidden = lax.dot_general(dhi[...], octant_ref[...], NT, preferred_element_type=F32)
    dhidden = dhidden + lax.dot_general(dlo[...], octant_ref[...], NT, preferred_element_type=F32)
    keeps = jnp.dot(mask_ref[...].astype(F32).astype(BF16), spread_ref[...], preferred_element_type=F32)

    blank = jnp.zeros((width, STRIDE - SPAN), F32)
    for block in range(blocks):
        rows = slice(block * width, (block + 1) * width)
        pre = pre_ref[rows, :]
        gate = 1.0 / (1.0 + jnp.exp(-pre))
        dpre = dhidden[rows] * keeps[block : block + 1] * gate * (1.0 + pre * (1.0 - gate))
        dpre = jnp.concatenate([dpre, blank], axis=1)
        lanes = slice(block * STRIDE, (block + 1) * STRIDE)
        for k in range(9):
            moved = pltpu.roll(dpre, (k // 3) * PLANE + (k % 3) * 8, 1) if k else dpre
            d9[k * width : (k + 1) * width, lanes] = moved.astype(BF16)

    part = jnp.dot(d9[...], patches_ref[...], preferred_element_type=F32)
    for k in range(27):
        conv_s[k * width : (k + 1) * width] = part[
            k // 3 * width : (k // 3 + 1) * width, k % 3 * channels : (k % 3 + 1) * channels
        ]
    half = keep_out.shape[0]
    keep_out[...] = conv_s[pl.ds(pl.multiple_of(core * half, 8), half), :]
    give_out[...] = conv_s[pl.ds(pl.multiple_of((1 - core) * half, 8), half), :]


def finish_kernel(axes, shards, half, own_ref, other_ref, conv_ref, down_ref, both):
    me = lax.axis_index(axes[1])
    core = lax.axis_index(axes[0]) & 1
    share = down_ref.shape[1]
    width = LANES // shards
    both[core] = own_ref[...]
    both[1 - core] = other_ref[...]
    conv_ref[:half] = both[0, :half]
    conv_ref[half:] = both[1, :half]
    group = lax.broadcasted_iota(jnp.int32, (share, LANES), 1) // width
    for octant in range(8):
        result = jnp.zeros((share, LANES), F32)
        for k in range(shards):
            source = me ^ k
            row = half + k * share
            tile = both[octant // shards, row : row + share, :]
            turned = pltpu.roll(tile, ((source - octant % shards + shards) & (shards - 1)) * width, 1)
            result = jnp.where(group == source, turned, result)
        down_ref[octant] = result


def exchange(values, axis, step):
    count = lax.axis_size(axis)
    return lax.ppermute(values, axis, [(i, i ^ step) for i in range(count)])


def local(features, voxel_mask, neighbors, w_conv, w_down, coarse_owner, cotangent):
    blocks, channels = features.shape[0], features.shape[1]
    edge = blocks // 2
    peers = lax.axis_size("space")
    shards = lax.axis_size("chan")
    axes = ("space", "chan")
    width = w_conv.shape[1]
    total = w_down.shape[1]
    share = total // shards
    capacity = cotangent.shape[0] // peers
    lanes = blocks * 64

    head, tail, packed = pl.pallas_call(
        prepare_kernel,
        grid=(1,),
        out_shape=[
            jax.ShapeDtypeStruct((edge // 2, channels, LANES), BF16),
            jax.ShapeDtypeStruct((edge // 2, channels, LANES), BF16),
            jax.ShapeDtypeStruct((peers, share, capacity * 64), BF16),
        ],
        in_specs=[
            pl.BlockSpec((edge, channels, LANES), lambda i: (0, 0, 0)),
            pl.BlockSpec((edge, channels, LANES), lambda i: (1, 0, 3)),
            pl.BlockSpec(voxel_mask.shape, lambda i: (0, 0)),
            pl.BlockSpec(cotangent.shape, lambda i: (0, 0, 0)),
        ],
        out_specs=[
            pl.BlockSpec((edge // 2, channels, LANES), lambda i: (0, 0, 0)),
            pl.BlockSpec((edge // 2, channels, LANES), lambda i: (0, 0, 0)),
            pl.BlockSpec((peers, share, capacity * 64), lambda i: (0, 0, 0)),
        ],
        cost_estimate=cost(2),
        compiler_params=pltpu.CompilerParams(vmem_limit_bytes=60 * MIB),
    )(features, features, voxel_mask, cotangent)
    ends = peers - 1
    before = lax.ppermute(tail, "space", [(i, i + 1) for i in range(ends)])
    after = lax.ppermute(head, "space", [(i + 1, i) for i in range(ends)])
    returned = lax.all_to_all(packed, "space", split_axis=0, concat_axis=0, tiled=True)

    dpiece, place = pl.pallas_call(
        pick_kernel,
        out_shape=[
            jax.ShapeDtypeStruct((share, lanes), BF16),
            jax.ShapeDtypeStruct((blocks, LANES), jnp.int32),
        ],
        in_specs=[vmem()] * 2,
        out_specs=[vmem()] * 2,
        cost_estimate=cost(1.5),
        compiler_params=pltpu.CompilerParams(vmem_limit_bytes=8 * MIB),
    )(coarse_owner.reshape(1, blocks), returned)
    dpieces = [dpiece] + [exchange(dpiece, "chan", k) for k in range(1, shards)]

    pre, octs, patches, spreads, octants = pl.pallas_call(
        functools.partial(forward_kernel, "chan"),
        out_shape=[
            jax.ShapeDtypeStruct((blocks * width, SPAN), F32),
            jax.ShapeDtypeStruct((8 * width, lanes), BF16),
            jax.ShapeDtypeStruct((blocks * STRIDE, 3 * channels), BF16),
            jax.ShapeDtypeStruct((512, SPAN), BF16),
            jax.ShapeDtypeStruct((SPAN, 8 * 64), BF16),
        ],
        in_specs=[vmem()] * 2 + [pl.BlockSpec(memory_space=pltpu.HBM)] * 4,
        out_specs=[vmem()] * 5,
        scratch_shapes=[
            pltpu.VMEM((11 * blocks + 1, channels, LANES), BF16),
            pltpu.VMEM((9 * width, 3 * channels), BF16),
            pltpu.VMEM((blocks * width, 512), BF16),
            pltpu.VMEM((blocks * width, SPAN), BF16),
            pltpu.SMEM((8 * blocks + 8,), jnp.int32),
            pltpu.SMEM((8 * blocks + 8,), jnp.int32),
            pltpu.SMEM((18 * blocks + 8,), jnp.int32),
            pltpu.SMEM((18 * blocks + 8,), jnp.int32),
            pltpu.SMEM(neighbors.shape, jnp.int32),
            pltpu.VMEM(features.shape, BF16),
            pltpu.VMEM(voxel_mask.shape, jnp.int32),
            pltpu.VMEM(w_conv.shape, BF16),
            pltpu.VMEM((10, LANES, LANES), BF16),
            pltpu.VMEM((3 * 2 * PLANE, 2 * LANES), BF16),
            pltpu.SemaphoreType.DMA((4,)),
        ],
        cost_estimate=cost(8),
        compiler_params=pltpu.CompilerParams(vmem_limit_bytes=40 * MIB),
    )(before, after, neighbors, features, voxel_mask, w_conv)

    pieces, down_grad, dp_all = pl.pallas_call(
        functools.partial(down_kernel, axes, shards),
        out_shape=[
            jax.ShapeDtypeStruct((shards, share, lanes), F32),
            jax.ShapeDtypeStruct((shards, 2, share, LANES), F32),
            jax.ShapeDtypeStruct((total, lanes), BF16),
        ],
        in_specs=[vmem()] * (2 + shards),
        out_specs=[vmem()] * 3,
        scratch_shapes=[pltpu.VMEM((8 * channels, lanes), BF16), pltpu.VMEM((total, lanes), F32)],
        cost_estimate=cost(1),
        compiler_params=pltpu.CompilerParams(vmem_limit_bytes=24 * MIB),
    )(octs, w_down, *dpieces)
    downs = [down_grad[0]] + [exchange(down_grad[k], "chan", k) for k in range(1, shards)]
    parts = [pieces[0]] + [exchange(pieces[k], "chan", k) for k in range(1, shards)]

    half = 27 * width // 2
    conv_keep, conv_give = pl.pallas_call(
        functools.partial(backward_kernel, axes),
        out_shape=[jax.ShapeDtypeStruct((half, channels), F32)] * 2,
        in_specs=[vmem()] * 7,
        out_specs=[vmem()] * 2,
        scratch_shapes=[
            pltpu.VMEM((8, channels, lanes), F32),
            pltpu.VMEM((blocks * width, 8 * 64), BF16),
            pltpu.VMEM((blocks * width, 8 * 64), BF16),
            pltpu.VMEM((9 * width, blocks * STRIDE), BF16),
            pltpu.VMEM((27 * width, channels), F32),
        ],
        cost_estimate=cost(6),
        compiler_params=pltpu.CompilerParams(vmem_limit_bytes=40 * MIB),
    )(dp_all, w_down, voxel_mask, pre, spreads, octants, patches)

    outgoing = pl.pallas_call(
        route_kernel,
        out_shape=jax.ShapeDtypeStruct((peers, share, capacity * 64), BF16),
        in_specs=[vmem()] * (1 + shards),
        out_specs=vmem(),
        cost_estimate=cost(1.5),
        compiler_params=pltpu.CompilerParams(vmem_limit_bytes=8 * MIB),
    )(place, *parts)
    coarse = lax.all_to_all(outgoing, "space", split_axis=0, concat_axis=0, tiled=True)
    coarse = coarse.reshape(peers, share, capacity, 64).transpose(0, 2, 1, 3).reshape(peers * capacity, share, 64)

    keep = jnp.concatenate([conv_keep] + [d[0] for d in downs])
    give = jnp.concatenate([conv_give] + [d[1] for d in downs])
    mine = keep + exchange(give, "space", 1)
    step = 2
    while step < peers:
        mine = mine + exchange(mine, "space", step)
        step *= 2
    other = exchange(mine, "space", 1)
    conv_sum, down_sum = pl.pallas_call(
        functools.partial(finish_kernel, axes, shards, half),
        out_shape=[
            jax.ShapeDtypeStruct((27 * width, channels), F32),
            jax.ShapeDtypeStruct((8, share, channels), F32),
        ],
        in_specs=[vmem(), vmem()],
        out_specs=[vmem()] * 2,
        scratch_shapes=[pltpu.VMEM((2,) + mine.shape, F32)],
        cost_estimate=cost(1.5),
        compiler_params=pltpu.CompilerParams(vmem_limit_bytes=8 * MIB),
    )(mine, other)
    return coarse, conv_sum.reshape(27, width, channels), down_sum


def solution(mesh):
    in_specs = (
        P("space", None, None),
        P("space", None),
        P("space", None),
        P(None, "chan", None),
        P(),
        P("space", None),
        P("space", "chan", None),
    )
    out_specs = (P("space", "chan", None), P(None, "chan", None), P(None, "chan", None))
    return jax.shard_map(local, mesh=mesh, in_specs=in_specs, out_specs=out_specs, check_vma=False)
```

```python
import functools

import jax
import jax.numpy as jnp
from jax import lax
from jax.experimental import pallas as pl
from jax.experimental.pallas import tpu as pltpu
from jax.sharding import PartitionSpec as P

F32 = jnp.float32
BF16 = jnp.bfloat16
SIGNS = (-1, 0, 1)
LANES = 128
NT = (((1,), (1,)), ((), ()))
TN = (((0,), (0,)), ((), ()))
MIB = 1024 * 1024
PLANE = 80
STRIDE = 896
SPAN = 640


def vmem():
    return pl.BlockSpec(memory_space=pltpu.VMEM)


def cost(microseconds):
    return pl.CostEstimate(flops=int(microseconds * 1.15e9), bytes_accessed=0, transcendentals=0)


def rim_lane(cell_y, cell_z):
    high_y, high_z = (cell_y > 0).astype(jnp.int32), (cell_z > 0).astype(jnp.int32)
    own_y, own_z = (cell_y >= 0) & (cell_y < 8), (cell_z >= 0) & (cell_z < 8)
    edges = jnp.where(own_z, 64 + 8 * high_y + cell_z, 80 + 8 * high_z + cell_y)
    lane = jnp.where(own_y & own_z, 8 * cell_y + cell_z, edges)
    return jnp.where(own_y | own_z, lane, 96 + 2 * high_y + high_z)


def column(rows):
    return lax.broadcasted_iota(jnp.int32, (rows, 1), 0)


def row(lanes):
    return lax.broadcasted_iota(jnp.int32, (1, lanes), 1)


def equal(left, right):
    return jnp.where(left == right, 1.0, 0.0).astype(BF16)


def edge_table(step_y, step_z):
    source = column(LANES)
    far_y, far_z = (source >> 3) + 8 * step_y, (source & 7) + 8 * step_z
    there = (source < 64) & (far_y >= -1) & (far_y <= 8) & (far_z >= -1) & (far_z <= 8)
    return equal(jnp.where(there, rim_lane(far_y, far_z), -1), row(LANES))


def shift_table(step_z):
    cell = column(2 * PLANE)
    plane = (cell >= PLANE).astype(jnp.int32)
    cell = cell - plane * PLANE
    lane = rim_lane((cell >> 3) - 1, (cell & 7) + step_z)
    return equal(plane * LANES + lane, row(2 * LANES))


def spread_table():
    voxel = column(512)
    return equal((voxel >> 6) * PLANE + (voxel & 63), row(SPAN))


def octant_table(plane):
    cell = column(PLANE)
    octant = 4 * (plane % 2) + 2 * ((cell >> 3) & 1) + (cell & 1)
    place = 16 * (plane // 2) + 4 * ((cell >> 4) & 3) + ((cell >> 1) & 3)
    return equal(jnp.where(cell < 64, octant * 64 + place, -1), row(8 * 64))


def low_half(rows):
    return lax.broadcasted_iota(jnp.int32, (rows, LANES), 1) < 64


def swap_halves(tile):
    return pltpu.roll(tile, 64, 1)


def prepare_kernel(head_ref, tail_ref, mask_ref, cot_ref, head_out, tail_out, cot_out):
    edge, channels = head_ref.shape[0], head_ref.shape[1]
    low = low_half(channels)
    for pair in range(edge // 2):
        one, two = 2 * pair, 2 * pair + 1
        first = head_ref[one].astype(F32) * mask_ref[one : one + 1, :LANES].astype(F32)
        second = head_ref[two].astype(F32) * mask_ref[two : two + 1, :LANES].astype(F32)
        head_out[pair] = jnp.where(low, first, swap_halves(second)).astype(BF16)
        first = tail_ref[one].astype(F32) * mask_ref[edge + one : edge + one + 1, -LANES:].astype(F32)
        second = tail_ref[two].astype(F32) * mask_ref[edge + two : edge + two + 1, -LANES:].astype(F32)
        tail_out[pair] = jnp.where(low, swap_halves(first), second).astype(BF16)
    for peer in range(cot_out.shape[0]):
        pair = [cot_ref[2 * peer].astype(F32), cot_ref[2 * peer + 1].astype(F32)]
        cot_out[peer] = jnp.concatenate(pair, axis=1).astype(BF16)


def pick_kernel(owner_ref, returned_ref, out_ref, slot_ref):
    blocks = owner_ref.shape[1]
    share = out_ref.shape[0]
    low = low_half(share)
    owners = owner_ref[...].astype(F32)
    block = lax.broadcasted_iota(jnp.int32, (blocks, blocks), 0)
    other = lax.broadcasted_iota(jnp.int32, (blocks, blocks), 1)
    owner = jnp.sum(jnp.where(block == other, owners, 0.0), axis=1, keepdims=True)
    rank = jnp.sum(jnp.where((owner == owners) & (other < block), 1.0, 0.0), axis=1, keepdims=True)
    slots = jnp.broadcast_to((2.0 * owner + rank).astype(jnp.int32), (blocks, LANES))
    slot_ref[...] = slots
    sources = [returned_ref[peer].astype(F32) for peer in range(returned_ref.shape[0])]
    for pair in range(blocks // 2):
        tiles = []
        for side in range(2):
            slot = jnp.broadcast_to(slots[2 * pair + side : 2 * pair + side + 1], (share, LANES))
            tile = sources[0]
            for peer in range(1, len(sources)):
                tile = jnp.where((slot >> 1) == peer, sources[peer], tile)
            tiles.append(jnp.where((slot & 1) == side, tile, swap_halves(tile)))
        out_ref[:, pair * LANES : (pair + 1) * LANES] = jnp.where(low, tiles[0], tiles[1]).astype(BF16)


def route_kernel(slot_ref, *refs):
    out_ref = refs[-1]
    blocks, share = slot_ref.shape[0], out_ref.shape[1]
    half = lax.broadcasted_iota(jnp.int32, (share, LANES), 1) // 64
    pieces = []
    for block in range(blocks):
        lanes = slice(block // 2 * LANES, (block // 2 + 1) * LANES)
        total = refs[0][:, lanes]
        for ref in refs[1:-1]:
            total = total + ref[:, lanes]
        slot = jnp.broadcast_to(slot_ref[block : block + 1, :], (share, LANES))
        rank = slot & 1
        tile = jnp.where(rank == block % 2, total, swap_halves(total))
        pieces.append((jnp.where(half == rank, slot >> 1, -1), tile))
    for peer in range(out_ref.shape[0]):
        tile = jnp.zeros((share, LANES), F32)
        for owner, piece in pieces:
            tile = jnp.where(owner == peer, piece, tile)
        out_ref[peer] = tile.astype(BF16)


def forward_kernel(
    axis,
    prev_ref,
    next_ref,
    nbr_hbm,
    feat_hbm,
    mask_hbm,
    wconv_hbm,
    pre_out,
    octs_out,
    patches_out,
    spread_ref,
    octant_ref,
    planes,
    weights,
    own_s,
    hidden_s,
    same_list,
    side_list,
    nbr_ref,
    feat_ref,
    mask_ref,
    wconv_ref,
    edge_ref,
    shift_ref,
    sems,
):
    loads = [
        pltpu.make_async_copy(source, target, sems.at[i])
        for i, (source, target) in enumerate(
            [
                (nbr_hbm, nbr_ref),
                (mask_hbm, mask_ref),
                (feat_hbm, feat_ref),
                (wconv_hbm, wconv_ref),
            ]
        )
    ]
    for load in loads:
        load.start()
    blocks, channels = feat_ref.shape[0], feat_ref.shape[1]
    edge = blocks // 2
    width = wconv_ref.shape[1]
    me = lax.axis_index(axis)
    own_rows = pl.ds(pl.multiple_of(me * width, width), width)
    low = low_half(channels)
    halo = 10 * blocks
    dummy = 11 * blocks

    for table in range(9):
        edge_ref[table] = edge_table(table // 3 - 1, table % 3 - 1)
    edge_ref[9] = jnp.zeros((LANES, LANES), BF16)
    for j in range(3):
        shift_ref[j * 2 * PLANE : (j + 1) * 2 * PLANE, :] = shift_table(j - 1)
    spread_ref[...] = spread_table()
    for plane in range(8):
        octant_ref[plane * PLANE : (plane + 1) * PLANE, :] = octant_table(plane)

    loads[0].wait()
    same, side = jnp.int32(0), jnp.int32(0)
    for block in range(blocks):
        for column in range(26):
            position = column + (column >= 13)
            source = nbr_ref[block, column]
            there = (source >= 0).astype(jnp.int32)
            step, table = position // 9, position % 9
            if step == 1:
                same_list[same] = source * 256 + (block * 16 + table)
                same = same + there
            else:
                side_list[side] = source * 4096 + ((block * 10 + (9 if step else 0)) * 32 + table * 2 + step // 2)
                side = side + there

    loads[1].wait()
    loads[2].wait()
    def two_planes(first, tile):
        planes[first] = jnp.where(low, tile, 0.0).astype(BF16)
        planes[first + 1] = jnp.where(low, swap_halves(tile), 0.0).astype(BF16)

    zero_plane = jnp.zeros((channels, LANES), BF16)
    planes[dummy] = zero_plane
    for block in range(blocks):
        keep = mask_ref[block : block + 1, :].astype(F32)
        masked = feat_ref[block].astype(F32) * keep
        planes[10 * block] = zero_plane
        planes[10 * block + 9] = zero_plane
        for pair in range(4):
            two_planes(10 * block + 1 + 2 * pair, masked[:, pair * LANES : (pair + 1) * LANES])
    for pair in range(edge // 2):
        two_planes(halo + 2 * pair, prev_ref[pair].astype(F32))
        two_planes(halo + edge + 2 * pair, next_ref[pair].astype(F32))

    same_list[same] = 9

    def same_layer(item, carry):
        results = []
        for extra in range(2):
            entry = same_list[2 * item + extra]
            source, code = entry >> 8, entry & 255
            cells = planes[pl.ds(source * 10 + 1, 8)].reshape(8 * channels, LANES)
            moved = jnp.dot(cells, edge_ref[code & 15], preferred_element_type=F32).astype(BF16)
            results.append((lax.shift_right_logical(code, 4), moved.reshape(8, channels, LANES)))
        for block, moved in results:
            planes[pl.ds(block * 10 + 1, 8)] += moved
        return carry

    lax.fori_loop(0, lax.shift_right_logical(same + 1, 1), same_layer, 0)
    for extra in range(3):
        side_list[side + extra] = (dummy - halo + blocks) * 4096 + dummy * 32 + 18

    def side_layer(item, carry):
        results = []
        for extra in range(4):
            entry = side_list[4 * item + extra]
            source, code = entry >> 12, entry & 4095
            own = source * 10 + jnp.where(code & 1 == 1, 1, 8)
            cells = planes[jnp.where(source < blocks, own, halo + source - blocks)]
            table = edge_ref[lax.shift_right_logical(code, 1) & 15]
            moved = jnp.dot(cells, table, preferred_element_type=F32).astype(BF16)
            results.append((lax.shift_right_logical(code, 5), moved))
        for place, moved in results:
            planes[place] += moved
        return carry

    lax.fori_loop(0, lax.shift_right_logical(side + 3, 2), side_layer, 0)

    loads[3].wait()
    for k in range(27):
        weights[(k // 3) * width : (k // 3 + 1) * width, (k % 3) * channels : (k % 3 + 1) * channels] = wconv_ref[k]

    for block in range(0, blocks, 2):
        for plane in range(0, 10, 2):
            first, second = block * 10 + plane, block * 10 + 10 + plane
            source = jnp.concatenate(
                [
                    jnp.concatenate([planes[first], planes[first + 1]], axis=1),
                    jnp.concatenate([planes[second], planes[second + 1]], axis=1),
                ],
                axis=0,
            )
            window = lax.dot_general(shift_ref[...], source, NT, preferred_element_type=F32).astype(BF16)
            for j in range(3):
                for half in range(2):
                    row = (block + half) * STRIDE + plane * PLANE
                    patches_out[row : row + 2 * PLANE, j * channels : (j + 1) * channels] = window[
                        j * 2 * PLANE : (j + 1) * 2 * PLANE, half * channels : (half + 1) * channels
                    ]
    for block in range(blocks):
        row = block * STRIDE + 10 * PLANE
        patches_out[row : (block + 1) * STRIDE, :] = jnp.zeros((STRIDE - 10 * PLANE, 3 * channels), BF16)

    for block in range(blocks):
        own_s[block * width : (block + 1) * width, :] = feat_ref[block, own_rows, :]
    own = jnp.dot(own_s[...], spread_ref[...], preferred_element_type=F32)
    keeps = jnp.dot(mask_ref[...].astype(F32).astype(BF16), spread_ref[...], preferred_element_type=F32)
    for block in range(blocks):
        rows = slice(block * STRIDE, (block + 1) * STRIDE)
        here = slice(block * width, (block + 1) * width)
        sums = lax.dot_general(weights[...], patches_out[rows, :], NT, preferred_element_type=F32)
        keep = keeps[block : block + 1]
        pre = own[here] * keep + sums[:width, :SPAN]
        for k in range(1, 9):
            moved = pltpu.roll(sums[k * width : (k + 1) * width], STRIDE - (k // 3) * PLANE - (k % 3) * 8, 1)
            pre = pre + moved[:, :SPAN]
        pre_out[here, :] = pre
        hidden_s[here, :] = (keep * (pre * (1.0 / (1.0 + jnp.exp(-pre))))).astype(BF16)

    split_up = jnp.dot(hidden_s[...], octant_ref[...], preferred_element_type=F32)
    low = low_half(width)
    for octant in range(0, 8, 2):
        lanes = slice(octant * 64, octant * 64 + LANES)
        for pair in range(blocks // 2):
            even = split_up[2 * pair * width : (2 * pair + 1) * width, lanes]
            odd = split_up[(2 * pair + 1) * width : (2 * pair + 2) * width, lanes]
            at = slice(pair * LANES, (pair + 1) * LANES)
            first = jnp.where(low, even, swap_halves(odd)).astype(BF16)
            second = jnp.where(low, swap_halves(even), odd).astype(BF16)
            octs_out[octant * width : (octant + 1) * width, at] = first
            octs_out[(octant + 1) * width : (octant + 2) * width, at] = second


def down_kernel(axes, shards, octs_ref, wdown_ref, *refs):
    dps = refs[:shards]
    pieces_out, grads_out, dp_out, spread, sums = refs[shards:]
    me = lax.axis_index(axes[1])
    core = lax.axis_index(axes[0]) & 1
    channels, total = wdown_ref.shape[2], wdown_ref.shape[1]
    width = channels // shards
    share = total // shards
    for k in range(shards):
        theirs = pl.multiple_of((me ^ k) * share, share)
        dp_out[pl.ds(theirs, share), :] = dps[k][...]
    grads = lax.dot_general(dp_out[...], octs_ref[...], NT, preferred_element_type=F32)
    sums[:, : 2 * LANES] = grads
    for k in range(shards):
        rows = pl.ds(pl.multiple_of((me ^ k) * share, share), share)
        low, high = sums[rows, :LANES], sums[rows, LANES : 2 * LANES]
        grads_out[k, core] = low
        grads_out[k, 1 - core] = high
    spread[...] = jnp.zeros_like(spread)
    for octant in range(8):
        rows = pl.ds(pl.multiple_of(octant * channels + me * width, width), width)
        spread[rows, :] = octs_ref[octant * width : (octant + 1) * width, :]
    down_weights = jnp.concatenate([wdown_ref[octant] for octant in range(8)], axis=1)
    sums[...] = jnp.dot(down_weights, spread[...], preferred_element_type=F32)
    for k in range(shards):
        pieces_out[k] = sums[pl.ds(pl.multiple_of((me ^ k) * share, share), share), :]


def backward_kernel(
    axes, dp_ref, wdown_ref, mask_ref, pre_ref, spread_ref, octant_ref, patches_ref, keep_out, give_out, dh_s, dhi, dlo, d9, conv_s
):
    blocks = mask_ref.shape[0]
    channels = wdown_ref.shape[2]
    width = pre_ref.shape[0] // blocks
    me = lax.axis_index(axes[1])
    core = lax.axis_index(axes[0]) & 1
    own_rows = pl.ds(pl.multiple_of(me * width, width), width)
    low = low_half(width)

    for octant in range(8):
        dh_s[octant] = lax.dot_general(wdown_ref[octant], dp_ref[...], TN, preferred_element_type=F32)
    for octant in range(0, 8, 2):
        lanes = slice(octant * 64, octant * 64 + LANES)
        for pair in range(blocks // 2):
            at = slice(pair * LANES, (pair + 1) * LANES)
            first, second = dh_s[octant, own_rows, at], dh_s[octant + 1, own_rows, at]
            for block, tile in (
                (2 * pair, jnp.where(low, first, swap_halves(second))),
                (2 * pair + 1, jnp.where(low, swap_halves(first), second)),
            ):
                rows = slice(block * width, (block + 1) * width)
                high = tile.astype(BF16)
                dhi[rows, lanes] = high
                dlo[rows, lanes] = (tile - high.astype(F32)).astype(BF16)
    dhidden = lax.dot_general(dhi[...], octant_ref[...], NT, preferred_element_type=F32)
    dhidden = dhidden + lax.dot_general(dlo[...], octant_ref[...], NT, preferred_element_type=F32)
    keeps = jnp.dot(mask_ref[...].astype(F32).astype(BF16), spread_ref[...], preferred_element_type=F32)

    blank = jnp.zeros((width, STRIDE - SPAN), F32)
    for block in range(blocks):
        rows = slice(block * width, (block + 1) * width)
        pre = pre_ref[rows, :]
        gate = 1.0 / (1.0 + jnp.exp(-pre))
        dpre = dhidden[rows] * keeps[block : block + 1] * gate * (1.0 + pre * (1.0 - gate))
        dpre = jnp.concatenate([dpre, blank], axis=1).astype(BF16)
        lanes = slice(block * STRIDE, (block + 1) * STRIDE)
        for k in range(9):
            moved = pltpu.roll(dpre, (k // 3) * PLANE + (k % 3) * 8, 1) if k else dpre
            d9[k * width : (k + 1) * width, lanes] = moved

    part = jnp.dot(d9[...], patches_ref[...], preferred_element_type=F32)
    for k in range(27):
        conv_s[k * width : (k + 1) * width] = part[
            k // 3 * width : (k // 3 + 1) * width, k % 3 * channels : (k % 3 + 1) * channels
        ]
    half = keep_out.shape[0]
    keep_out[...] = conv_s[pl.ds(pl.multiple_of(core * half, 8), half), :]
    give_out[...] = conv_s[pl.ds(pl.multiple_of((1 - core) * half, 8), half), :]


def finish_kernel(axes, shards, half, own_ref, other_ref, conv_ref, down_ref, both):
    me = lax.axis_index(axes[1])
    core = lax.axis_index(axes[0]) & 1
    share = down_ref.shape[1]
    width = LANES // shards
    both[core] = own_ref[...]
    both[1 - core] = other_ref[...]
    conv_ref[:half] = both[0, :half]
    conv_ref[half:] = both[1, :half]
    group = lax.broadcasted_iota(jnp.int32, (share, LANES), 1) // width
    for octant in range(8):
        result = jnp.zeros((share, LANES), F32)
        for k in range(shards):
            source = me ^ k
            row = half + k * share
            tile = both[octant // shards, row : row + share, :]
            turned = pltpu.roll(tile, ((source - octant % shards + shards) & (shards - 1)) * width, 1)
            result = jnp.where(group == source, turned, result)
        down_ref[octant] = result


def exchange(values, axis, step):
    count = lax.axis_size(axis)
    return lax.ppermute(values, axis, [(i, i ^ step) for i in range(count)])


def local(features, voxel_mask, neighbors, w_conv, w_down, coarse_owner, cotangent):
    blocks, channels = features.shape[0], features.shape[1]
    edge = blocks // 2
    peers = lax.axis_size("space")
    shards = lax.axis_size("chan")
    axes = ("space", "chan")
    width = w_conv.shape[1]
    total = w_down.shape[1]
    share = total // shards
    capacity = cotangent.shape[0] // peers
    lanes = blocks * 64

    head, tail, packed = pl.pallas_call(
        prepare_kernel,
        grid=(1,),
        out_shape=[
            jax.ShapeDtypeStruct((edge // 2, channels, LANES), BF16),
            jax.ShapeDtypeStruct((edge // 2, channels, LANES), BF16),
            jax.ShapeDtypeStruct((peers, share, capacity * 64), BF16),
        ],
        in_specs=[
            pl.BlockSpec((edge, channels, LANES), lambda i: (0, 0, 0)),
            pl.BlockSpec((edge, channels, LANES), lambda i: (1, 0, 3)),
            pl.BlockSpec(voxel_mask.shape, lambda i: (0, 0)),
            pl.BlockSpec(cotangent.shape, lambda i: (0, 0, 0)),
        ],
        out_specs=[
            pl.BlockSpec((edge // 2, channels, LANES), lambda i: (0, 0, 0)),
            pl.BlockSpec((edge // 2, channels, LANES), lambda i: (0, 0, 0)),
            pl.BlockSpec((peers, share, capacity * 64), lambda i: (0, 0, 0)),
        ],
        cost_estimate=cost(2),
        compiler_params=pltpu.CompilerParams(vmem_limit_bytes=60 * MIB),
    )(features, features, voxel_mask, cotangent)
    ends = peers - 1
    before = lax.ppermute(tail, "space", [(i, i + 1) for i in range(ends)])
    after = lax.ppermute(head, "space", [(i + 1, i) for i in range(ends)])
    returned = lax.all_to_all(packed, "space", split_axis=0, concat_axis=0, tiled=True)

    dpiece, place = pl.pallas_call(
        pick_kernel,
        out_shape=[
            jax.ShapeDtypeStruct((share, lanes), BF16),
            jax.ShapeDtypeStruct((blocks, LANES), jnp.int32),
        ],
        in_specs=[vmem()] * 2,
        out_specs=[vmem()] * 2,
        cost_estimate=cost(1.5),
        compiler_params=pltpu.CompilerParams(vmem_limit_bytes=8 * MIB),
    )(coarse_owner.reshape(1, blocks), returned)
    dpieces = [dpiece] + [exchange(dpiece, "chan", k) for k in range(1, shards)]

    pre, octs, patches, spreads, octants = pl.pallas_call(
        functools.partial(forward_kernel, "chan"),
        out_shape=[
            jax.ShapeDtypeStruct((blocks * width, SPAN), F32),
            jax.ShapeDtypeStruct((8 * width, lanes), BF16),
            jax.ShapeDtypeStruct((blocks * STRIDE, 3 * channels), BF16),
            jax.ShapeDtypeStruct((512, SPAN), BF16),
            jax.ShapeDtypeStruct((SPAN, 8 * 64), BF16),
        ],
        in_specs=[vmem()] * 2 + [pl.BlockSpec(memory_space=pltpu.HBM)] * 4,
        out_specs=[vmem()] * 5,
        scratch_shapes=[
            pltpu.VMEM((11 * blocks + 1, channels, LANES), BF16),
            pltpu.VMEM((9 * width, 3 * channels), BF16),
            pltpu.VMEM((blocks * width, 512), BF16),
            pltpu.VMEM((blocks * width, SPAN), BF16),
            pltpu.SMEM((8 * blocks + 8,), jnp.int32),
            pltpu.SMEM((18 * blocks + 8,), jnp.int32),
            pltpu.SMEM(neighbors.shape, jnp.int32),
            pltpu.VMEM(features.shape, BF16),
            pltpu.VMEM(voxel_mask.shape, jnp.int32),
            pltpu.VMEM(w_conv.shape, BF16),
            pltpu.VMEM((10, LANES, LANES), BF16),
            pltpu.VMEM((3 * 2 * PLANE, 2 * LANES), BF16),
            pltpu.SemaphoreType.DMA((4,)),
        ],
        cost_estimate=cost(8),
        compiler_params=pltpu.CompilerParams(vmem_limit_bytes=40 * MIB),
    )(before, after, neighbors, features, voxel_mask, w_conv)

    pieces, down_grad, dp_all = pl.pallas_call(
        functools.partial(down_kernel, axes, shards),
        out_shape=[
            jax.ShapeDtypeStruct((shards, share, lanes), F32),
            jax.ShapeDtypeStruct((shards, 2, share, LANES), F32),
            jax.ShapeDtypeStruct((total, lanes), BF16),
        ],
        in_specs=[vmem()] * (2 + shards),
        out_specs=[vmem()] * 3,
        scratch_shapes=[pltpu.VMEM((8 * channels, lanes), BF16), pltpu.VMEM((total, lanes), F32)],
        cost_estimate=cost(1),
        compiler_params=pltpu.CompilerParams(vmem_limit_bytes=24 * MIB),
    )(octs, w_down, *dpieces)
    downs = [down_grad[0]] + [exchange(down_grad[k], "chan", k) for k in range(1, shards)]
    parts = [pieces[0]] + [exchange(pieces[k], "chan", k) for k in range(1, shards)]

    half = 27 * width // 2
    conv_keep, conv_give = pl.pallas_call(
        functools.partial(backward_kernel, axes),
        out_shape=[jax.ShapeDtypeStruct((half, channels), F32)] * 2,
        in_specs=[vmem()] * 7,
        out_specs=[vmem()] * 2,
        scratch_shapes=[
            pltpu.VMEM((8, channels, lanes), F32),
            pltpu.VMEM((blocks * width, 8 * 64), BF16),
            pltpu.VMEM((blocks * width, 8 * 64), BF16),
            pltpu.VMEM((9 * width, blocks * STRIDE), BF16),
            pltpu.VMEM((27 * width, channels), F32),
        ],
        cost_estimate=cost(6),
        compiler_params=pltpu.CompilerParams(vmem_limit_bytes=40 * MIB),
    )(dp_all, w_down, voxel_mask, pre, spreads, octants, patches)

    outgoing = pl.pallas_call(
        route_kernel,
        out_shape=jax.ShapeDtypeStruct((peers, share, capacity * 64), BF16),
        in_specs=[vmem()] * (1 + shards),
        out_specs=vmem(),
        cost_estimate=cost(1.5),
        compiler_params=pltpu.CompilerParams(vmem_limit_bytes=8 * MIB),
    )(place, *parts)
    coarse = lax.all_to_all(outgoing, "space", split_axis=0, concat_axis=0, tiled=True)
    coarse = coarse.reshape(peers, share, capacity, 64).transpose(0, 2, 1, 3).reshape(peers * capacity, share, 64)

    keep = jnp.concatenate([conv_keep] + [d[0] for d in downs])
    give = jnp.concatenate([conv_give] + [d[1] for d in downs])
    mine = keep + exchange(give, "space", 1)
    step = 2
    while step < peers:
        mine = mine + exchange(mine, "space", step)
        step *= 2
    other = exchange(mine, "space", 1)
    conv_sum, down_sum = pl.pallas_call(
        functools.partial(finish_kernel, axes, shards, half),
        out_shape=[
            jax.ShapeDtypeStruct((27 * width, channels), F32),
            jax.ShapeDtypeStruct((8, share, channels), F32),
        ],
        in_specs=[vmem(), vmem()],
        out_specs=[vmem()] * 2,
        scratch_shapes=[pltpu.VMEM((2,) + mine.shape, F32)],
        cost_estimate=cost(1.5),
        compiler_params=pltpu.CompilerParams(vmem_limit_bytes=8 * MIB),
    )(mine, other)
    return coarse, conv_sum.reshape(27, width, channels), down_sum


def solution(mesh):
    in_specs = (
        P("space", None, None),
        P("space", None),
        P("space", None),
        P(None, "chan", None),
        P(),
        P("space", None),
        P("space", "chan", None),
    )
    out_specs = (P("space", "chan", None), P(None, "chan", None), P(None, "chan", None))
    return jax.shard_map(local, mesh=mesh, in_specs=in_specs, out_specs=out_specs, check_vma=False)
```
